128 devices in a mesh: dp: 16 (over y, x_lo, core), narrow: 8 (over z, x_hi).
Axes of the slice: x: 4 (x_hi: 2, x_lo: 2; x = x_hi * 2 + x_lo), y: 4, z: 4, core: 2. Of those that a mesh axis runs over, the one named last changes fastest.
Arguments:
- embeddings: bfloat16 [262144, 128], P(('dp', 'narrow')), may hold values from -6 to 6
- cluster_id: int32 [262144], P(('dp', 'narrow')), may hold values from 0 to 31, as said below
- member_rank: int32 [262144], P(('dp', 'narrow')), may hold values from 0 to 12287, as said below
- cluster_size: int32 [32], replicated, may hold values from 4096 to 12288, as said below
- cluster_owner: int32 [32], replicated, may hold values from 0 to 15, as said below
Outputs:
- similar: float32 [262144], P(('dp', 'narrow'))
The draws below stay inside these ranges and needn't reach their ends.
Inputs may be any that keep to these rules, and one draw needn't show every extreme that they name: `member_rank`: ranks of one cluster are 0 to its size - 1, each held by exactly one row; a cluster of owner g occupies the slots g * 2048 * 8 + offset + rank, where offset is the total size of the clusters of the same owner with smaller ids; slot s lies with device s // 2048 of the mesh order. `cluster_id`: of the rows of one device, at most 32 have slots on any one device, and exactly 32 for some pair of devices. `cluster_size`: the sizes of the clusters of one owner sum to 2048 * 8. `cluster_owner`: every group owns exactly 2 clusters.
All inputs are finite; a program needn't handle non-finite values.
Results may differ from the reference program's by a relative error of at most 0.0013.
Values may be sent and summed in bfloat16 or wider, within the bound.
A program may use at most 64 MiB of HBM per device.

```python
import jax
import jax.numpy as jnp
from jax import lax

EMB = 128
ROWS_DEV = 2048
CL_GROUP = 2
ROWS = 262144
CLUSTERS = 32
N_DP = 16
N_NARROW = 8
DEVICES = 128


def layout(key):
    subkeys = jax.random.split(key, 6)
    group_rows = ROWS_DEV * N_NARROW
    quarter = group_rows // 4
    cluster_ids = jnp.arange(CLUSTERS, dtype=jnp.int32)
    order = jax.random.permutation(subkeys[0], CLUSTERS).astype(jnp.int32)
    owner = (order // CL_GROUP).astype(jnp.int32)
    same_owner = owner[None, :] == owner[:, None]
    position = jnp.sum(same_owner & (cluster_ids[None, :] < cluster_ids[:, None]), axis=1).astype(jnp.int32)
    spread = jax.random.randint(subkeys[1], (N_DP,), 0, quarter + 1).astype(jnp.int32).at[0].set(quarter)
    sizes_all = jnp.where(position == 0, 2 * quarter + spread[owner], 2 * quarter - spread[owner]).astype(jnp.int32)
    table = jnp.zeros((N_DP, CL_GROUP), jnp.int32).at[owner, position].set(cluster_ids)
    slot_index = jnp.arange(ROWS, dtype=jnp.int32)
    group_index = slot_index // group_rows
    inner = slot_index % group_rows
    split_at = 2 * quarter + spread[group_index]
    second = (inner >= split_at).astype(jnp.int32)
    slot_cluster = table[group_index, second]
    slot_rank = inner - second * split_at
    share = ROWS_DEV // DEVICES
    swing = jax.random.randint(subkeys[2], (DEVICES // 2,), 0, share + 1).astype(jnp.int32).at[0].set(share)
    shifts = jnp.stack([swing, -swing], axis=1).reshape(DEVICES)[jax.random.permutation(subkeys[3], DEVICES)]
    src_ids = jnp.arange(DEVICES, dtype=jnp.int32)
    counts = share + shifts[(src_ids[None, :] - src_ids[:, None]) % DEVICES]
    row_cum = jnp.cumsum(counts, axis=1)
    col_before = jnp.cumsum(counts, axis=0) - counts
    src_order = jax.vmap(lambda sub: jax.random.permutation(sub, ROWS_DEV))(jax.random.split(subkeys[4], DEVICES)).astype(jnp.int32)
    dst_order = jax.vmap(lambda sub: jax.random.permutation(sub, ROWS_DEV))(jax.random.split(subkeys[5], DEVICES)).astype(jnp.int32)
    targets = jax.vmap(lambda cumul, query: jnp.searchsorted(cumul, query, side='right'))(row_cum, src_order).astype(jnp.int32)
    source = jnp.broadcast_to(src_ids[:, None], targets.shape)
    start_col = row_cum[source, targets] - counts[source, targets]
    arrival = col_before[source, targets] + src_order - start_col
    final_slot = (targets * ROWS_DEV + dst_order[targets, arrival]).reshape(-1)
    return (slot_cluster[final_slot], slot_rank[final_slot], sizes_all, owner)


def draw_cluster_id(key, part):
    return layout(key)[0]


def draw_member_rank(key, part):
    return layout(key)[1]


def draw_cluster_size(key, part):
    return layout(key)[2]


def draw_cluster_owner(key, part):
    return layout(key)[3]


def shard_levels(own_key, shape, cuts, smallest, largest):
    def one(dim, shards_of):
        steps = jax.random.uniform(jax.random.fold_in(jax.random.fold_in(own_key, 6), dim), (shards_of,), jnp.float32, smallest / len(cuts), largest / len(cuts))
        return jnp.repeat(jnp.exp(steps), shape[dim] // shards_of).reshape((-1,) + (1,) * (len(shape) - dim - 1))

    loudness = one(*cuts[0])
    for cut in cuts[1:]:
        loudness = loudness * one(*cut)
    return loudness


def bell_draw(own_key, shape, deviation, limit, shards=(), held_as=jnp.bfloat16):
    values = jax.random.normal(own_key, shape, jnp.float32) * deviation
    if len(shards) > 0:
        values = shard_levels(own_key, shape, shards, -0.22, 0.18) * values
    return jnp.clip(values, min=-limit, max=limit).astype(held_as)


def setup_inputs(seed: int = 0) -> dict:
    splits = jax.random.split(jax.random.key(seed), 6)
    embeddings = bell_draw(splits[0], (ROWS, EMB), 1.0, 6.0, ((0, 128),))
    cluster_id = draw_cluster_id(jax.random.fold_in(splits[5], 71), 0)
    member_rank = draw_member_rank(jax.random.fold_in(splits[5], 71), 0)
    cluster_size = draw_cluster_size(jax.random.fold_in(splits[5], 71), 0)
    cluster_owner = draw_cluster_owner(jax.random.fold_in(splits[5], 71), 0)
    return {"embeddings": embeddings, "cluster_id": cluster_id, "member_rank": member_rank, "cluster_size": cluster_size, "cluster_owner": cluster_owner}


def reference(embeddings, cluster_id, member_rank, cluster_size, cluster_owner):
    widened = embeddings.astype(jnp.float32)
    normed = (widened * lax.rsqrt(lax.optimization_barrier(jnp.sum(widened * widened, axis=1, keepdims=True)) + 1e-06)).astype(jnp.bfloat16)
    cluster_ids = jnp.arange(CLUSTERS, dtype=jnp.int32)
    same_owner = cluster_owner[None, :] == cluster_owner[:, None]
    earlier_ids = same_owner & (cluster_ids[None, :] < cluster_ids[:, None])
    offset = lax.optimization_barrier(jnp.sum(jnp.where(earlier_ids, cluster_size[None, :], 0), axis=1)).astype(jnp.int32)
    group_rows = ROWS_DEV * N_NARROW
    target = (cluster_owner[cluster_id] * group_rows + offset[cluster_id] + member_rank).astype(jnp.int32)
    ordered = jnp.zeros((ROWS, EMB), jnp.float32).at[target].set(normed.astype(jnp.float32))
    labels = jnp.zeros((ROWS,), jnp.int32).at[target].set(cluster_id)
    block_rows = min(512, group_rows)
    grouped = ordered.reshape(N_DP, group_rows, EMB)
    grouped_labels = labels.reshape(N_DP, group_rows)
    slot_index = jnp.arange(group_rows, dtype=jnp.int32)

    def per_group(operands):
        embed_group, label_group = operands

        def per_block(block_index):
            first_row = (block_index * block_rows).astype(jnp.int32)
            row_block = lax.dynamic_slice_in_dim(embed_group, first_row, block_rows, 0)
            label_block = lax.dynamic_slice_in_dim(label_group, first_row, block_rows, 0)
            slot_block = first_row + jnp.arange(block_rows, dtype=jnp.int32)
            scores = jnp.dot(row_block, embed_group.T, precision=lax.Precision.HIGHEST)
            allowed = (slot_index[None, :] < slot_block[:, None]) & (label_group[None, :] == label_block[:, None])
            return jnp.maximum(-1.0, lax.optimization_barrier(jnp.max(jnp.where(allowed, scores, -1.0), axis=1)))
        return lax.map(per_block, jnp.arange(group_rows // block_rows, dtype=jnp.int32)).reshape(-1)
    result = lax.map(per_group, (grouped, grouped_labels)).reshape(-1)
    return result[target]
```

```python
import jax
import jax.numpy as jnp
from jax import lax
from jax.experimental import pallas as pl
from jax.experimental.pallas import tpu as pltpu
from jax.sharding import PartitionSpec as P

MESH = pl.DeviceIdType.MESH
NT = (((1,), (1,)), ((), ()))
DEV = 128
CAP = 32
ROWS = 2048
EMB = 128
CHUNKS = 4
CROWS = ROWS // CHUNKS
BF = jnp.bfloat16
F32 = jnp.float32
I32 = jnp.int32


def div(a, b):
    return lax.div(a, jnp.int32(b))


def rem(a, b):
    return lax.rem(a, jnp.int32(b))


def place(x, y, z, core):
    return (y * 4 + rem(x, 2) * 2 + core, z * 2 + div(x, 2))


def place_of(index):
    member = rem(index, 8)
    group = div(index, 8)
    return place(rem(group, 4), div(group, 4), div(member, 2), rem(member, 2))


def split3(value):
    high = value.astype(BF)
    rest = value - high.astype(F32)
    middle = rest.astype(BF)
    low = (rest - middle.astype(F32)).astype(BF)
    return jnp.concatenate([high, middle, low], axis=0)


def kernel(
    emb_ref, cid_ref, rank_ref, size_ref, owner_ref, out_ref,
    normed, bucket, arrived, slot_out, slot_in, dest_hot, dest_row, pos_row, flat_row,
    total, blocks, row_feat, col_feat, best, part_out, part_in, table, answer, answer_in, turned,
    send_slot, recv_slot, send_row, recv_row, send_block, recv_block, send_part, recv_part, send_ans, recv_ans,
):
    dp = lax.axis_index("dp")
    nar = lax.axis_index("narrow")
    y, core = div(dp, 4), rem(dp, 2)
    x = rem(nar, 2) * 2 + rem(div(dp, 2), 2)
    z = div(nar, 2)
    group = y * 4 + x
    member = z * 2 + core
    me = group * 8 + member
    quarter = rem(me, 4) * CAP

    barrier = pltpu.get_barrier_semaphore()

    def greet(i, carry):
        pl.semaphore_signal(barrier, inc=1, device_id=place_of(rem(me + i, DEV)), device_id_type=MESH)
        return carry

    lax.fori_loop(1, DEV, greet, 0)

    cid = cid_ref[...]

    def owners(j, carry):
        owner, bound, seen = carry
        own = owner_ref[j]
        owner = jnp.where(cid == j, own, owner)
        mine = own == group
        bound = jnp.where(mine & (seen == 0), size_ref[j], bound)
        seen = jnp.where(mine, 1, seen)
        return owner, bound, seen

    owner, bound, _ = lax.fori_loop(
        0, 32, owners, (jnp.zeros((1, ROWS), I32), jnp.int32(0), jnp.int32(0))
    )

    def offsets(j, offset):
        return offset + jnp.where((owner == owner_ref[j]) & (cid > j), size_ref[j], 0)

    offset = lax.fori_loop(0, 32, offsets, rank_ref[...])
    dest = owner * 8 + (offset >> 11)
    local = offset & (ROWS - 1)
    dest_row[...] = dest

    hot = dest == lax.broadcasted_iota(I32, (DEV, ROWS), 0)
    dest_hot[...] = jnp.where(hot, 1.0, 0.0).astype(BF)
    upper = jnp.where(
        lax.broadcasted_iota(I32, (256, 256), 0) <= lax.broadcasted_iota(I32, (256, 256), 1), 1.0, 0.0
    ).astype(BF)
    before = jnp.full((DEV, 1), -1.0, F32)
    for k in range(ROWS // 256):
        piece = dest_hot[:, k * 256:(k + 1) * 256]
        count = jnp.dot(piece, upper, preferred_element_type=F32)
        position = jnp.sum(jnp.where(piece.astype(F32) > 0.5, count + before, 0.0), axis=0, keepdims=True)
        pos_row[:, k * 256:(k + 1) * 256] = position.astype(I32)
        before = before + count[:, 255:256]
    pos = pos_row[...]
    flat_row[...] = dest * CAP + pos

    lane_hot = (pos + quarter) == lax.broadcasted_iota(I32, (DEV, ROWS), 0)
    code = local + 1
    high = jnp.where(lane_hot, (code & ~63).astype(F32), 0.0).astype(BF)
    low = jnp.where(lane_hot, (code & 63).astype(F32), 0.0).astype(BF)
    codes = lax.dot_general(dest_hot[...], high, NT, preferred_element_type=F32)
    codes = codes + lax.dot_general(dest_hot[...], low, NT, preferred_element_type=F32)
    slot_out[...] = codes.astype(I32).reshape(DEV, 1, 128)

    pl.semaphore_wait(barrier, DEV - 1)

    def send_slots(i, carry):
        to = rem(me + i, DEV)
        pltpu.make_async_remote_copy(
            src_ref=slot_out.at[to], dst_ref=slot_in.at[me], send_sem=send_slot, recv_sem=recv_slot,
            device_id=place_of(to), device_id_type=MESH,
        ).start()
        return carry

    lax.fori_loop(1, DEV, send_slots, 0)
    pltpu.make_async_copy(slot_out.at[me], slot_in.at[me], recv_slot).start()

    wide = emb_ref[...].astype(F32)
    normed[...] = (wide * lax.rsqrt(jnp.sum(wide * wide, axis=1, keepdims=True) + 1e-06)).astype(BF)

    flip_x = 1 - 2 * rem(x, 2)
    flip_y = 1 - 2 * rem(y, 2)

    def partner(i):
        px = rem(x + flip_x * rem(i, 4) + 4, 4)
        py = rem(y + flip_y * div(i, 4) + 4, 4)
        return py * 4 + px

    def fill(other):
        wanted = other * 256 + lax.broadcasted_iota(I32, (256, ROWS), 0)
        pick = jnp.where(flat_row[...] == wanted, 1.0, 0.0).astype(BF)
        rows = jnp.dot(pick, normed[...], preferred_element_type=F32)
        bucket[pl.ds(pl.multiple_of(other * 256, 256), 256), :] = rows.astype(BF)

    def send_rows(other, j):
        to = other * 8 + rem(member + j, 8)
        pltpu.make_async_remote_copy(
            src_ref=bucket.at[pl.ds(pl.multiple_of(to * CAP, CAP), CAP)],
            dst_ref=arrived.at[pl.ds(pl.multiple_of(me * CAP, CAP), CAP)],
            send_sem=send_row, recv_sem=recv_row.at[group],
            device_id=place_of(to), device_id_type=MESH,
        ).start()

    def dispatch(i, carry):
        other = partner(i)
        fill(other)
        for j in range(8):
            send_rows(other, j)
        return carry

    lax.fori_loop(1, 16, dispatch, 0)
    fill(group)
    for j in range(1, 8):
        send_rows(group, j)
    mine = pl.ds(pl.multiple_of(me * CAP, CAP), CAP)
    pltpu.make_async_copy(bucket.at[mine], arrived.at[mine], recv_row.at[group]).start()

    up = rem(z + 1, 4)
    down = rem(z + 3, 4)
    first_lane = lax.broadcasted_iota(I32, (256, EMB), 1) == 0
    numbers = (member, up * 2 + core, down * 2 + core, up * 2 + 1 - core)
    for b in range(4):
        def features(t, carry):
            at = pl.ds(pl.multiple_of(t * 256, 256), 256)
            slot = numbers[b] * ROWS + t * 256 + lax.broadcasted_iota(I32, (256, EMB), 0)
            late = slot >= bound
            row_feat[b, at, :] = jnp.where(first_lane & late, 1.0, 0.0).astype(BF)
            col_feat[b, at, :] = jnp.where(first_lane & jnp.logical_not(late), -8.0, 0.0).astype(BF)
            return carry

        lax.fori_loop(0, 8, features, 0)
    best[...] = jnp.full((4, 8, ROWS), -1.0, F32)

    total[...] = jnp.zeros((ROWS, EMB), F32)
    pltpu.make_async_copy(slot_in, slot_in, recv_slot).wait()

    def codes_of(k):
        return jnp.sum(slot_in[pl.ds(4 * k, 4)], axis=0)

    def compact(i, carry):
        other = partner(rem(i, 16))
        at = pl.ds(pl.multiple_of(other * 256, 256), 256)
        pltpu.make_async_copy(arrived.at[at], arrived.at[at], recv_row.at[other]).wait()
        code_row = jnp.concatenate([codes_of(2 * other), codes_of(2 * other + 1)], axis=1)
        rows = arrived[at, :]
        for m in range(4):
            wanted = lax.broadcasted_iota(I32, (512, 256), 0) + (m * 512 + 1)
            pick = jnp.where(code_row == wanted, 1.0, 0.0).astype(BF)
            total[m * 512:(m + 1) * 512, :] += jnp.dot(pick, rows, preferred_element_type=F32)
        return carry

    lax.fori_loop(1, 17, compact, 0)
    blocks[0] = total[...].astype(BF)

    def block_copy(src, dst, ch, to):
        rows = pl.ds(ch * CROWS, CROWS)
        return pltpu.make_async_remote_copy(
            src_ref=blocks.at[src, rows], dst_ref=blocks.at[dst, rows],
            send_sem=send_block.at[dst], recv_sem=recv_block.at[dst, ch],
            device_id=to, device_id_type=MESH,
        )

    above = place(x, y, up, core)
    below = place(x, y, down, core)
    beside = place(x, y, z, 1 - core)
    above_beside = place(x, y, up, 1 - core)
    for ch in range(CHUNKS):
        block_copy(0, 1, ch, below).start()
        block_copy(0, 2, ch, above).start()

    def tile(row_block, rt, col_block, ct, diagonal):
        rat = pl.ds(pl.multiple_of(rt * 256, 256), 256)
        width = 256 if diagonal else 512
        cat = pl.ds(pl.multiple_of(ct * width, width), width)
        rows = jnp.concatenate([blocks[row_block, rat, :], row_feat[row_block, rat, :]], axis=1)
        cols = jnp.concatenate([blocks[col_block, cat, :], col_feat[col_block, cat, :]], axis=1)
        scores = lax.dot_general(cols, rows, NT, preferred_element_type=F32)
        if diagonal:
            c = lax.broadcasted_iota(I32, (width, 256), 0) + ct * 256
            r = lax.broadcasted_iota(I32, (width, 256), 1) + rt * 256
            scores = jnp.where(c < r, scores, -1.0)
        top = jnp.max(scores.reshape(width // 8, 8, 256), axis=0)
        best[row_block, :, rat] = jnp.maximum(best[row_block, :, rat], top)

    def triangle(rt, carry):
        def inner(ct, carry):
            tile(0, rt, 0, ct, True)
            return carry

        return lax.fori_loop(0, rt + 1, inner, carry)

    lax.fori_loop(0, 8, triangle, 0)

    def later(p, q):
        return jnp.where(numbers[q] > numbers[p], 1, 0)

    def pair_chunk(p, q, ch):
        flag = later(p, q)
        row_block = flag * q + (1 - flag) * p
        col_block = flag * p + (1 - flag) * q

        def unit(u, carry):
            rt = flag * (ch * 2 + rem(u, 2)) + (1 - flag) * u
            ct = flag * div(u, 2) + (1 - flag) * ch
            tile(row_block, rt, col_block, ct, False)
            return carry

        lax.fori_loop(0, 8, unit, 0)

    def pair_half(p, q, half):
        flag = later(p, q)
        row_block = flag * q + (1 - flag) * p
        col_block = flag * p + (1 - flag) * q

        def unit(u, carry):
            tile(row_block, div(u, 2), col_block, half * 2 + rem(u, 2), False)
            return carry

        lax.fori_loop(0, 16, unit, 0)

    for ch in range(CHUNKS):
        block_copy(0, 1, ch, below).wait_recv()
        block_copy(1, 3, ch, beside).start()
        pair_chunk(0, 1, ch)
    for ch in range(CHUNKS):
        block_copy(0, 2, ch, above).wait_recv()
    pair_half(1, 2, div(z, 2))
    for ch in range(CHUNKS):
        block_copy(1, 3, ch, beside).wait_recv()
        pair_chunk(0, 3, ch)
    pair_half(1, 3, core)
    pair_half(2, 3, core)

    whole = blocks.at[0]
    for dst in (1, 2, 3):
        part_out[dst] = jnp.max(best[dst], axis=0, keepdims=True)
        pltpu.make_async_remote_copy(
            src_ref=part_out.at[dst], dst_ref=part_in.at[dst], send_sem=send_part.at[dst], recv_sem=recv_part.at[dst],
            device_id=(None, above, below, above_beside)[dst], device_id_type=MESH,
        ).start()
    top = jnp.max(best[0], axis=0, keepdims=True)
    for dst in (1, 2, 3):
        pltpu.make_async_copy(part_in.at[dst], part_in.at[dst], recv_part.at[dst]).wait()
        top = jnp.maximum(top, part_in[dst])

    for k in range(16):
        table[k:k + 1, :] = top[:, k * 128:(k + 1) * 128]
    values = split3(table[...])
    for part in range(4):
        index = jnp.concatenate([codes_of(part * 8 + k) for k in range(8)], axis=1) - 1
        fine = jnp.where((index & 127) == lax.broadcasted_iota(I32, (128, 1024), 0), 1.0, 0.0).astype(BF)
        found = jnp.dot(values, fine, preferred_element_type=F32)
        found = (found[0:16] + found[16:32]) + found[32:48]
        coarse = (index >> 7) == lax.broadcasted_iota(I32, (16, 1024), 0)
        line = jnp.sum(jnp.where(coarse, found, 0.0), axis=0, keepdims=True)
        for k in range(8):
            answer[part * 8 + k] = line[:, k * 128:(k + 1) * 128]

    def send_answers(i, carry):
        to = rem(me + i, DEV)
        pltpu.make_async_remote_copy(
            src_ref=answer.at[div(to, 4)], dst_ref=answer_in.at[me], send_sem=send_ans, recv_sem=recv_ans,
            device_id=place_of(to), device_id_type=MESH,
        ).start()
        return carry

    lax.fori_loop(1, DEV, send_answers, 0)
    pltpu.make_async_copy(answer.at[div(me, 4)], answer_in.at[me], recv_ans).start()
    pltpu.make_async_copy(answer_in, answer_in, recv_ans).wait()

    turned[...] = answer_in[...].reshape(DEV, 128).T
    mine_back = split3(turned[pl.ds(pl.multiple_of(quarter, CAP), CAP), :])
    back = jnp.dot(mine_back, dest_hot[...], preferred_element_type=F32)
    back = (back[0:32] + back[32:64]) + back[64:96]
    spot = pos_row[...] == lax.broadcasted_iota(I32, (CAP, ROWS), 0)
    out_ref[...] = jnp.sum(jnp.where(spot, back, 0.0), axis=0, keepdims=True)

    others = pl.ds(0, DEV - 1)
    pltpu.make_async_copy(slot_in.at[others], slot_in.at[others], send_slot).wait()
    pltpu.make_async_copy(answer_in.at[others], answer_in.at[others], send_ans).wait()
    sent = pl.ds(0, (DEV - 1) * CAP)
    pltpu.make_async_copy(arrived.at[sent], arrived.at[sent], send_row).wait()
    for dst in (1, 2, 3):
        pltpu.make_async_copy(whole, whole, send_block.at[dst]).wait()
        pltpu.make_async_copy(part_in.at[dst], part_in.at[dst], send_part.at[dst]).wait()


def shards(embeddings, cluster_id, member_rank, cluster_size, cluster_owner):
    vmem = pl.BlockSpec(memory_space=pltpu.VMEM)
    smem = pl.BlockSpec(memory_space=pltpu.SMEM)
    dma = pltpu.SemaphoreType.DMA
    result = pl.pallas_call(
        kernel,
        out_shape=jax.ShapeDtypeStruct((1, ROWS), F32),
        in_specs=[vmem, vmem, vmem, smem, smem],
        out_specs=vmem,
        scratch_shapes=[
            pltpu.VMEM((ROWS, EMB), BF),
            pltpu.VMEM((DEV * CAP, EMB), BF),
            pltpu.VMEM((DEV * CAP, EMB), BF),
            pltpu.VMEM((DEV, 1, 128), I32),
            pltpu.VMEM((DEV, 1, 128), I32),
            pltpu.VMEM((DEV, ROWS), BF),
            pltpu.VMEM((1, ROWS), I32),
            pltpu.VMEM((1, ROWS), I32),
            pltpu.VMEM((1, ROWS), I32),
            pltpu.VMEM((ROWS, EMB), F32),
            pltpu.VMEM((4, ROWS, EMB), BF),
            pltpu.VMEM((4, ROWS, EMB), BF),
            pltpu.VMEM((4, ROWS, EMB), BF),
            pltpu.VMEM((4, 8, ROWS), F32),
            pltpu.VMEM((4, 1, ROWS), F32),
            pltpu.VMEM((4, 1, ROWS), F32),
            pltpu.VMEM((16, 128), F32),
            pltpu.VMEM((32, 1, 128), F32),
            pltpu.VMEM((DEV, 1, 128), F32),
            pltpu.VMEM((128, DEV), F32),
            dma, dma, dma, dma((16,)), dma((4,)), dma((4, CHUNKS)), dma((4,)), dma((4,)), dma, dma,
        ],
        compiler_params=pltpu.CompilerParams(
            collective_id=0, has_side_effects=True, vmem_limit_bytes=48 * 1024 * 1024
        ),
        cost_estimate=pl.CostEstimate(flops=12 * 10**9, bytes_accessed=1 << 20, transcendentals=2048),
    )(embeddings, cluster_id.reshape(1, ROWS), member_rank.reshape(1, ROWS), cluster_size, cluster_owner)
    return result.reshape(ROWS)


def solution(mesh):
    in_specs = (P(("dp", "narrow"), None), P(("dp", "narrow")), P(("dp", "narrow")), P(), P())
    out_specs = P(("dp", "narrow"))
    return jax.shard_map(shards, mesh=mesh, in_specs=in_specs, out_specs=out_specs, check_vma=False)
```

```python
import jax
import jax.numpy as jnp
from jax import lax
from jax.experimental import pallas as pl
from jax.experimental.pallas import tpu as pltpu
from jax.sharding import PartitionSpec as P

MESH = pl.DeviceIdType.MESH
NT = (((1,), (1,)), ((), ()))
DEV = 128
CAP = 32
ROWS = 2048
EMB = 128
CHUNKS = 4
CROWS = ROWS // CHUNKS
BF = jnp.bfloat16
F32 = jnp.float32
I32 = jnp.int32


def div(a, b):
    return lax.div(a, jnp.int32(b))


def rem(a, b):
    return lax.rem(a, jnp.int32(b))


def place(x, y, z, core):
    return (y * 4 + rem(x, 2) * 2 + core, z * 2 + div(x, 2))


def split3(value):
    high = value.astype(BF)
    rest = value - high.astype(F32)
    middle = rest.astype(BF)
    low = (rest - middle.astype(F32)).astype(BF)
    return jnp.concatenate([high, middle, low], axis=0)


def kernel(
    emb_hbm, cid_hbm, rank_hbm, size_hbm, owner_hbm, out_ref,
    emb_ref, cid_ref, rank_ref, size_ref, owner_ref, load_sem,
    normed, bucket, arrived, slot_out, slot_in, dest_hot, dest_row, pos_row, flat_row,
    total, blocks, row_feat, col_feat, best, part_out, part_in, table, answer, answer_in, turned,
    send_slot, recv_slot, send_row, recv_row, send_block, recv_block, send_part, recv_part, send_ans, recv_ans,
):
    dp = lax.axis_index("dp")
    nar = lax.axis_index("narrow")
    y, core = div(dp, 4), rem(dp, 2)
    x = rem(nar, 2) * 2 + rem(div(dp, 2), 2)
    z = div(nar, 2)
    group = y * 4 + x
    member = z * 2 + core
    me = dp * 8 + nar
    quarter = rem(me, 4) * CAP

    loads = [
        pltpu.make_async_copy(src, dst, load_sem.at[k])
        for k, (src, dst) in enumerate(
            ((owner_hbm, owner_ref), (size_hbm, size_ref), (cid_hbm, cid_ref), (rank_hbm, rank_ref), (emb_hbm, emb_ref))
        )
    ]
    for load in loads:
        load.start()

    barrier = pltpu.get_barrier_semaphore()

    def to_all(act):
        def line(i, carry):
            other = rem(dp + i, 16)
            for j in range(8):
                act(other, rem(nar + j, 8))
            return carry

        lax.fori_loop(1, 16, line, 0)
        for j in range(1, 8):
            act(dp, rem(nar + j, 8))

    def greet(other, column):
        pl.semaphore_signal(barrier, inc=1, device_id=(other, column), device_id_type=MESH)

    to_all(greet)
    for load in loads:
        load.wait()

    cid = cid_ref[...]

    def owners(j, carry):
        owner, bound, seen = carry
        own = owner_ref[j]
        owner = jnp.where(cid == j, own, owner)
        mine = own == group
        bound = jnp.where(mine & (seen == 0), size_ref[j], bound)
        seen = jnp.where(mine, 1, seen)
        return owner, bound, seen

    owner, bound, _ = lax.fori_loop(
        0, 32, owners, (jnp.zeros((1, ROWS), I32), jnp.int32(0), jnp.int32(0))
    )

    def offsets(j, offset):
        return offset + jnp.where((owner == owner_ref[j]) & (cid > j), size_ref[j], 0)

    offset = lax.fori_loop(0, 32, offsets, rank_ref[...])
    seat = offset >> 11
    dest = (
        ((owner >> 2) << 5) + ((owner & 1) << 4) + ((seat & 1) << 3) + ((seat >> 1) << 1) + ((owner >> 1) & 1)
    )
    local = offset & (ROWS - 1)
    dest_row[...] = dest

    hot = dest == lax.broadcasted_iota(I32, (DEV, ROWS), 0)
    dest_hot[...] = jnp.where(hot, 1.0, 0.0).astype(BF)
    upper = jnp.where(
        lax.broadcasted_iota(I32, (256, 256), 0) <= lax.broadcasted_iota(I32, (256, 256), 1), 1.0, 0.0
    ).astype(BF)
    before = jnp.full((DEV, 1), -1.0, F32)
    for k in range(ROWS // 256):
        piece = dest_hot[:, k * 256:(k + 1) * 256]
        count = jnp.dot(piece, upper, preferred_element_type=F32)
        position = jnp.sum(jnp.where(piece.astype(F32) > 0.5, count + before, 0.0), axis=0, keepdims=True)
        pos_row[:, k * 256:(k + 1) * 256] = position.astype(I32)
        before = before + count[:, 255:256]
    pos = pos_row[...]
    flat_row[...] = dest * CAP + pos

    lane_hot = (pos + quarter) == lax.broadcasted_iota(I32, (DEV, ROWS), 0)
    code = local + 1
    high = jnp.where(lane_hot, (code & ~63).astype(F32), 0.0).astype(BF)
    low = jnp.where(lane_hot, (code & 63).astype(F32), 0.0).astype(BF)
    codes = lax.dot_general(dest_hot[...], high, NT, preferred_element_type=F32)
    codes = codes + lax.dot_general(dest_hot[...], low, NT, preferred_element_type=F32)
    slot_out[...] = codes.astype(I32).reshape(DEV, 1, 128)

    pl.semaphore_wait(barrier, DEV - 1)

    wide = emb_ref[...].astype(F32)
    normed[...] = (wide * lax.rsqrt(jnp.sum(wide * wide, axis=1, keepdims=True) + 1e-06)).astype(BF)

    flip_y = 1 - 2 * rem(y, 2)
    half_x = rem(x, 2)

    def partner(i):
        k = rem(i * 7, 16)
        py = rem(y + flip_y * div(k, 4) + 4, 4)
        return py * 4 + rem(half_x + div(k, 2), 2) * 2 + rem(core + k, 2)

    def fill(other):
        wanted = other * 256 + lax.broadcasted_iota(I32, (256, ROWS), 0)
        pick = jnp.where(flat_row[...] == wanted, 1.0, 0.0).astype(BF)
        rows = jnp.dot(pick, normed[...], preferred_element_type=F32)
        bucket[pl.ds(pl.multiple_of(other * 256, 256), 256), :] = rows.astype(BF)

    def send_rows(other, j):
        column = rem(nar + j, 8)
        to = other * 8 + column
        pltpu.make_async_remote_copy(
            src_ref=slot_out.at[to], dst_ref=slot_in.at[me], send_sem=send_slot, recv_sem=recv_slot.at[dp],
            device_id=(other, column), device_id_type=MESH,
        ).start()
        pltpu.make_async_remote_copy(
            src_ref=bucket.at[pl.ds(pl.multiple_of(to * CAP, CAP), CAP)],
            dst_ref=arrived.at[pl.ds(pl.multiple_of(me * CAP, CAP), CAP)],
            send_sem=send_row, recv_sem=recv_row.at[dp],
            device_id=(other, column), device_id_type=MESH,
        ).start()

    def dispatch(i, carry):
        other = partner(i)
        fill(other)
        for j in range(8):
            send_rows(other, j)
        return carry

    lax.fori_loop(1, 16, dispatch, 0)
    fill(dp)
    for j in range(1, 8):
        send_rows(dp, j)
    mine = pl.ds(pl.multiple_of(me * CAP, CAP), CAP)
    pltpu.make_async_copy(slot_out.at[me], slot_in.at[me], recv_slot.at[dp]).start()
    pltpu.make_async_copy(bucket.at[mine], arrived.at[mine], recv_row.at[dp]).start()

    up = rem(z + 1, 4)
    down = rem(z + 3, 4)
    first_lane = lax.broadcasted_iota(I32, (256, EMB), 1) == 0
    numbers = (member, up * 2 + core, down * 2 + core, up * 2 + 1 - core)
    for b in range(4):
        def features(t, carry):
            at = pl.ds(pl.multiple_of(t * 256, 256), 256)
            slot = numbers[b] * ROWS + t * 256 + lax.broadcasted_iota(I32, (256, EMB), 0)
            late = slot >= bound
            row_feat[b, at, :] = jnp.where(first_lane & late, 1.0, 0.0).astype(BF)
            col_feat[b, at, :] = jnp.where(first_lane & jnp.logical_not(late), -8.0, 0.0).astype(BF)
            return carry

        lax.fori_loop(0, 8, features, 0)
    best[...] = jnp.full((4, 8, ROWS), -1.0, F32)

    total[...] = jnp.zeros((ROWS, EMB), F32)

    def codes_of(k):
        return jnp.sum(slot_in[pl.ds(4 * k, 4)], axis=0)

    def compact(i, carry):
        rows, codes = [], []
        for k in range(2):
            other = partner(rem(2 * i + 1 + k, 16))
            at = pl.ds(pl.multiple_of(other * 256, 256), 256)
            ats = pl.ds(pl.multiple_of(other * 8, 8), 8)
            pltpu.make_async_copy(slot_in.at[ats], slot_in.at[ats], recv_slot.at[other]).wait()
            pltpu.make_async_copy(arrived.at[at], arrived.at[at], recv_row.at[other]).wait()
            codes += [codes_of(2 * other), codes_of(2 * other + 1)]
            rows.append(arrived[at, :])
        code_row = jnp.concatenate(codes, axis=1)
        rows = jnp.concatenate(rows, axis=0)
        for m in range(4):
            wanted = lax.broadcasted_iota(I32, (512, 512), 0) + (m * 512 + 1)
            pick = jnp.where(code_row == wanted, 1.0, 0.0).astype(BF)
            total[m * 512:(m + 1) * 512, :] += jnp.dot(pick, rows, preferred_element_type=F32)
        return carry

    lax.fori_loop(0, 8, compact, 0)
    blocks[0] = total[...].astype(BF)

    def block_copy(src, dst, ch, to):
        rows = pl.ds(ch * CROWS, CROWS)
        return pltpu.make_async_remote_copy(
            src_ref=blocks.at[src, rows], dst_ref=blocks.at[dst, rows],
            send_sem=send_block.at[dst], recv_sem=recv_block.at[dst, ch],
            device_id=to, device_id_type=MESH,
        )

    above = place(x, y, up, core)
    below = place(x, y, down, core)
    beside = place(x, y, z, 1 - core)
    above_beside = place(x, y, up, 1 - core)
    for ch in range(CHUNKS):
        block_copy(0, 1, ch, below).start()
        block_copy(0, 2, ch, above).start()

    def tile(row_block, rt, col_block, ct, diagonal):
        rat = pl.ds(pl.multiple_of(rt * 256, 256), 256)
        width = 256 if diagonal else 512
        cat = pl.ds(pl.multiple_of(ct * width, width), width)
        rows = jnp.concatenate([blocks[row_block, rat, :], row_feat[row_block, rat, :]], axis=1)
        cols = jnp.concatenate([blocks[col_block, cat, :], col_feat[col_block, cat, :]], axis=1)
        scores = lax.dot_general(cols, rows, NT, preferred_element_type=F32)
        if diagonal:
            c = lax.broadcasted_iota(I32, (width, 256), 0) + ct * 256
            r = lax.broadcasted_iota(I32, (width, 256), 1) + rt * 256
            scores = jnp.where(c < r, scores, -1.0)
        top = jnp.max(scores.reshape(width // 8, 8, 256), axis=0)
        best[row_block, :, rat] = jnp.maximum(best[row_block, :, rat], top)

    def triangle(rt, carry):
        def inner(ct, carry):
            tile(0, rt, 0, ct, True)
            return carry

        return lax.fori_loop(0, rt + 1, inner, carry)

    lax.fori_loop(0, 8, triangle, 0)

    def later(p, q):
        return jnp.where(numbers[q] > numbers[p], 1, 0)

    def pair_chunk(p, q, ch):
        flag = later(p, q)
        row_block = flag * q + (1 - flag) * p
        col_block = flag * p + (1 - flag) * q

        def unit(u, carry):
            rt = flag * (ch * 2 + rem(u, 2)) + (1 - flag) * u
            ct = flag * div(u, 2) + (1 - flag) * ch
            tile(row_block, rt, col_block, ct, False)
            return carry

        lax.fori_loop(0, 8, unit, 0)

    def pair_half(p, q, half):
        flag = later(p, q)
        row_block = flag * q + (1 - flag) * p
        col_block = flag * p + (1 - flag) * q

        def unit(u, carry):
            tile(row_block, div(u, 2), col_block, half * 2 + rem(u, 2), False)
            return carry

        lax.fori_loop(0, 16, unit, 0)

    for ch in range(CHUNKS):
        block_copy(0, 1, ch, below).wait_recv()
        block_copy(1, 3, ch, beside).start()
        pair_chunk(0, 1, ch)
    for ch in range(CHUNKS):
        block_copy(0, 2, ch, above).wait_recv()
    pair_half(1, 2, div(z, 2))
    for ch in range(CHUNKS):
        block_copy(1, 3, ch, beside).wait_recv()
        pair_chunk(0, 3, ch)
    pair_half(1, 3, core)
    pair_half(2, 3, core)

    whole = blocks.at[0]
    for dst in (1, 2, 3):
        part_out[dst] = jnp.max(best[dst], axis=0, keepdims=True)
        pltpu.make_async_remote_copy(
            src_ref=part_out.at[dst], dst_ref=part_in.at[dst], send_sem=send_part.at[dst], recv_sem=recv_part.at[dst],
            device_id=(None, above, below, above_beside)[dst], device_id_type=MESH,
        ).start()
    top = jnp.max(best[0], axis=0, keepdims=True)
    for dst in (1, 2, 3):
        pltpu.make_async_copy(part_in.at[dst], part_in.at[dst], recv_part.at[dst]).wait()
        top = jnp.maximum(top, part_in[dst])

    for k in range(16):
        table[k:k + 1, :] = top[:, k * 128:(k + 1) * 128]
    values = split3(table[...])
    for part in range(4):
        index = jnp.concatenate([codes_of(part * 8 + k) for k in range(8)], axis=1) - 1
        fine = jnp.where((index & 127) == lax.broadcasted_iota(I32, (128, 1024), 0), 1.0, 0.0).astype(BF)
        found = jnp.dot(values, fine, preferred_element_type=F32)
        found = (found[0:16] + found[16:32]) + found[32:48]
        coarse = (index >> 7) == lax.broadcasted_iota(I32, (16, 1024), 0)
        line = jnp.sum(jnp.where(coarse, found, 0.0), axis=0, keepdims=True)
        for k in range(8):
            answer[part * 8 + k] = line[:, k * 128:(k + 1) * 128]

    def send_answer(other, column):
        pltpu.make_async_remote_copy(
            src_ref=answer.at[other * 2 + div(column, 4)], dst_ref=answer_in.at[me], send_sem=send_ans, recv_sem=recv_ans,
            device_id=(other, column), device_id_type=MESH,
        ).start()

    to_all(send_answer)
    pltpu.make_async_copy(answer.at[div(me, 4)], answer_in.at[me], recv_ans).start()
    pltpu.make_async_copy(answer_in, answer_in, recv_ans).wait()

    turned[...] = answer_in[...].reshape(DEV, 128).T
    mine_back = split3(turned[pl.ds(pl.multiple_of(quarter, CAP), CAP), :])
    back = jnp.dot(mine_back, dest_hot[...], preferred_element_type=F32)
    back = (back[0:32] + back[32:64]) + back[64:96]
    spot = pos_row[...] == lax.broadcasted_iota(I32, (CAP, ROWS), 0)
    out_ref[...] = jnp.sum(jnp.where(spot, back, 0.0), axis=0, keepdims=True)

    others = pl.ds(0, DEV - 1)
    pltpu.make_async_copy(slot_in.at[others], slot_in.at[others], send_slot).wait()
    pltpu.make_async_copy(answer_in.at[others], answer_in.at[others], send_ans).wait()
    sent = pl.ds(0, (DEV - 1) * CAP)
    pltpu.make_async_copy(arrived.at[sent], arrived.at[sent], send_row).wait()
    for dst in (1, 2, 3):
        pltpu.make_async_copy(whole, whole, send_block.at[dst]).wait()
        pltpu.make_async_copy(part_in.at[dst], part_in.at[dst], send_part.at[dst]).wait()


def shards(embeddings, cluster_id, member_rank, cluster_size, cluster_owner):
    vmem = pl.BlockSpec(memory_space=pltpu.VMEM)
    dma = pltpu.SemaphoreType.DMA
    result = pl.pallas_call(
        kernel,
        out_shape=jax.ShapeDtypeStruct((1, ROWS), F32),
        in_specs=[pl.BlockSpec(memory_space=pltpu.HBM)] * 5,
        out_specs=vmem,
        scratch_shapes=[
            pltpu.VMEM((ROWS, EMB), BF),
            pltpu.VMEM((1, ROWS), I32),
            pltpu.VMEM((1, ROWS), I32),
            pltpu.SMEM((32,), I32),
            pltpu.SMEM((32,), I32),
            dma((5,)),
            pltpu.VMEM((ROWS, EMB), BF),
            pltpu.VMEM((DEV * CAP, EMB), BF),
            pltpu.VMEM((DEV * CAP, EMB), BF),
            pltpu.VMEM((DEV, 1, 128), I32),
            pltpu.VMEM((DEV, 1, 128), I32),
            pltpu.VMEM((DEV, ROWS), BF),
            pltpu.VMEM((1, ROWS), I32),
            pltpu.VMEM((1, ROWS), I32),
            pltpu.VMEM((1, ROWS), I32),
            pltpu.VMEM((ROWS, EMB), F32),
            pltpu.VMEM((4, ROWS, EMB), BF),
            pltpu.VMEM((4, ROWS, EMB), BF),
            pltpu.VMEM((4, ROWS, EMB), BF),
            pltpu.VMEM((4, 8, ROWS), F32),
            pltpu.VMEM((4, 1, ROWS), F32),
            pltpu.VMEM((4, 1, ROWS), F32),
            pltpu.VMEM((16, 128), F32),
            pltpu.VMEM((32, 1, 128), F32),
            pltpu.VMEM((DEV, 1, 128), F32),
            pltpu.VMEM((128, DEV), F32),
            dma, dma((16,)), dma, dma((16,)), dma((4,)), dma((4, CHUNKS)), dma((4,)), dma((4,)), dma, dma,
        ],
        compiler_params=pltpu.CompilerParams(
            collective_id=0, has_side_effects=True, vmem_limit_bytes=62 * 1024 * 1024
        ),
        cost_estimate=pl.CostEstimate(flops=12 * 10**9, bytes_accessed=1 << 20, transcendentals=2048),
    )(embeddings, cluster_id.reshape(1, ROWS), member_rank.reshape(1, ROWS), cluster_size, cluster_owner)
    return result.reshape(ROWS)


def solution(mesh):
    in_specs = (P(("dp", "narrow"), None), P(("dp", "narrow")), P(("dp", "narrow")), P(), P())
    out_specs = P(("dp", "narrow"))
    return jax.shard_map(shards, mesh=mesh, in_specs=in_specs, out_specs=out_specs, check_vma=False)
```

```python
import jax
import jax.numpy as jnp
from jax import lax
from jax.experimental import pallas as pl
from jax.experimental.pallas import tpu as pltpu
from jax.sharding import PartitionSpec as P

MESH = pl.DeviceIdType.MESH
NT = (((1,), (1,)), ((), ()))
DEV = 128
CAP = 32
ROWS = 2048
EMB = 128
CHUNKS = 4
CROWS = ROWS // CHUNKS
BF = jnp.bfloat16
F32 = jnp.float32
I32 = jnp.int32


def div(a, b):
    return lax.div(a, jnp.int32(b))


def rem(a, b):
    return lax.rem(a, jnp.int32(b))


def place(x, y, z, core):
    return (y * 4 + rem(x, 2) * 2 + core, z * 2 + div(x, 2))


def split3(value):
    high = value.astype(BF)
    rest = value - high.astype(F32)
    middle = rest.astype(BF)
    low = (rest - middle.astype(F32)).astype(BF)
    return jnp.concatenate([high, middle, low], axis=0)


def kernel(
    emb_hbm, cid_hbm, rank_hbm, size_hbm, owner_hbm, out_ref,
    emb_ref, cid_ref, rank_ref, size_ref, owner_ref, load_sem,
    normed, bucket, arrived, slot_out, slot_in, dest_hot, dest_row, pos_row, flat_row,
    total, blocks, row_feat, col_feat, best, part_out, part_in, table, answer, answer_in, turned,
    send_slot, recv_slot, send_row, recv_row, send_block, recv_block, send_part, recv_part, send_ans, recv_ans,
):
    dp = lax.axis_index("dp")
    nar = lax.axis_index("narrow")
    y, core = div(dp, 4), rem(dp, 2)
    x = rem(nar, 2) * 2 + rem(div(dp, 2), 2)
    z = div(nar, 2)
    group = y * 4 + x
    member = z * 2 + core
    me = dp * 8 + nar
    quarter = rem(me, 4) * CAP

    loads = [
        pltpu.make_async_copy(src, dst, load_sem.at[k])
        for k, (src, dst) in enumerate(
            ((owner_hbm, owner_ref), (size_hbm, size_ref), (cid_hbm, cid_ref), (rank_hbm, rank_ref), (emb_hbm, emb_ref))
        )
    ]
    for load in loads:
        load.start()

    barrier = pltpu.get_barrier_semaphore()

    def to_all(act):
        def line(i, carry):
            other = rem(dp + i, 16)
            for j in range(8):
                act(other, rem(nar + j, 8))
            return carry

        lax.fori_loop(1, 16, line, 0)
        for j in range(1, 8):
            act(dp, rem(nar + j, 8))

    def greet(other, column):
        pl.semaphore_signal(barrier, inc=1, device_id=(other, column), device_id_type=MESH)

    to_all(greet)
    for load in loads:
        load.wait()

    cid = cid_ref[...]

    def owners(j, carry):
        owner, bound, seen = carry
        own = owner_ref[j]
        owner = jnp.where(cid == j, own, owner)
        mine = own == group
        bound = jnp.where(mine & (seen == 0), size_ref[j], bound)
        seen = jnp.where(mine, 1, seen)
        return owner, bound, seen

    owner, bound, _ = lax.fori_loop(
        0, 32, owners, (jnp.zeros((1, ROWS), I32), jnp.int32(0), jnp.int32(0))
    )

    def offsets(j, offset):
        return offset + jnp.where((owner == owner_ref[j]) & (cid > j), size_ref[j], 0)

    offset = lax.fori_loop(0, 32, offsets, rank_ref[...])
    seat = offset >> 11
    dest = (
        ((owner >> 2) << 5) + ((owner & 1) << 4) + ((seat & 1) << 3) + ((seat >> 1) << 1) + ((owner >> 1) & 1)
    )
    local = offset & (ROWS - 1)
    dest_row[...] = dest

    hot = dest == lax.broadcasted_iota(I32, (DEV, ROWS), 0)
    dest_hot[...] = jnp.where(hot, 1.0, 0.0).astype(BF)
    upper = jnp.where(
        lax.broadcasted_iota(I32, (256, 256), 0) <= lax.broadcasted_iota(I32, (256, 256), 1), 1.0, 0.0
    ).astype(BF)
    before = jnp.full((DEV, 1), -1.0, F32)
    for k in range(ROWS // 256):
        piece = dest_hot[:, k * 256:(k + 1) * 256]
        count = jnp.dot(piece, upper, preferred_element_type=F32)
        position = jnp.sum(jnp.where(piece.astype(F32) > 0.5, count + before, 0.0), axis=0, keepdims=True)
        pos_row[:, k * 256:(k + 1) * 256] = position.astype(I32)
        before = before + count[:, 255:256]
    pos = pos_row[...]
    flat_row[...] = dest * CAP + pos

    lane_hot = (pos + quarter) == lax.broadcasted_iota(I32, (DEV, ROWS), 0)
    code = local + 1
    high = jnp.where(lane_hot, (code & ~63).astype(F32), 0.0).astype(BF)
    low = jnp.where(lane_hot, (code & 63).astype(F32), 0.0).astype(BF)
    codes = lax.dot_general(dest_hot[...], high, NT, preferred_element_type=F32)
    codes = codes + lax.dot_general(dest_hot[...], low, NT, preferred_element_type=F32)
    slot_out[...] = codes.astype(I32).reshape(DEV, 1, 128)

    wide = emb_ref[...].astype(F32)
    normed[...] = (wide * lax.rsqrt(jnp.sum(wide * wide, axis=1, keepdims=True) + 1e-06)).astype(BF)

    pl.semaphore_wait(barrier, DEV - 1)

    flip_y = 1 - 2 * rem(y, 2)
    half_x = rem(x, 2)

    def partner(i):
        k = rem(i * 7, 16)
        py = rem(y + flip_y * div(k, 4) + 4, 4)
        return py * 4 + rem(half_x + div(k, 2), 2) * 2 + rem(core + k, 2)

    def fill(other):
        wanted = other * 256 + lax.broadcasted_iota(I32, (256, ROWS), 0)
        pick = jnp.where(flat_row[...] == wanted, 1.0, 0.0).astype(BF)
        rows = jnp.dot(pick, normed[...], preferred_element_type=F32)
        bucket[pl.ds(pl.multiple_of(other * 256, 256), 256), :] = rows.astype(BF)

    def send_rows(other, j):
        column = rem(nar + j, 8)
        to = other * 8 + column
        pltpu.make_async_remote_copy(
            src_ref=slot_out.at[to], dst_ref=slot_in.at[me], send_sem=send_slot, recv_sem=recv_slot.at[dp],
            device_id=(other, column), device_id_type=MESH,
        ).start()
        pltpu.make_async_remote_copy(
            src_ref=bucket.at[pl.ds(pl.multiple_of(to * CAP, CAP), CAP)],
            dst_ref=arrived.at[pl.ds(pl.multiple_of(me * CAP, CAP), CAP)],
            send_sem=send_row, recv_sem=recv_row.at[dp],
            device_id=(other, column), device_id_type=MESH,
        ).start()

    def dispatch(i, carry):
        other = partner(i)
        fill(other)
        for j in range(8):
            send_rows(other, j)
        return carry

    lax.fori_loop(1, 16, dispatch, 0)
    fill(dp)
    for j in range(1, 8):
        send_rows(dp, j)
    mine = pl.ds(pl.multiple_of(me * CAP, CAP), CAP)
    pltpu.make_async_copy(slot_out.at[me], slot_in.at[me], recv_slot.at[dp]).start()
    pltpu.make_async_copy(bucket.at[mine], arrived.at[mine], recv_row.at[dp]).start()

    up = rem(z + 1, 4)
    down = rem(z + 3, 4)
    first_lane = lax.broadcasted_iota(I32, (256, EMB), 1) == 0
    numbers = (member, up * 2 + core, down * 2 + core, up * 2 + 1 - core)
    for b in range(4):
        def features(t, carry):
            at = pl.ds(pl.multiple_of(t * 256, 256), 256)
            slot = numbers[b] * ROWS + t * 256 + lax.broadcasted_iota(I32, (256, EMB), 0)
            late = slot >= bound
            row_feat[b, at, :] = jnp.where(first_lane & late, 1.0, 0.0).astype(BF)
            col_feat[b, at, :] = jnp.where(first_lane & jnp.logical_not(late), -8.0, 0.0).astype(BF)
            return carry

        lax.fori_loop(0, 8, features, 0)
    best[...] = jnp.full((4, 8, ROWS), -1.0, F32)

    total[...] = jnp.zeros((ROWS, EMB), F32)

    def codes_of(k):
        return jnp.sum(slot_in[pl.ds(4 * k, 4)], axis=0)

    def compact(i, carry):
        rows, codes = [], []
        for k in range(2):
            other = partner(rem(2 * i + 1 + k, 16))
            at = pl.ds(pl.multiple_of(other * 256, 256), 256)
            ats = pl.ds(pl.multiple_of(other * 8, 8), 8)
            pltpu.make_async_copy(slot_in.at[ats], slot_in.at[ats], recv_slot.at[other]).wait()
            pltpu.make_async_copy(arrived.at[at], arrived.at[at], recv_row.at[other]).wait()
            codes += [codes_of(2 * other), codes_of(2 * other + 1)]
            rows.append(arrived[at, :])
        code_row = jnp.concatenate(codes, axis=1)
        rows = jnp.concatenate(rows, axis=0)
        for m in range(4):
            wanted = lax.broadcasted_iota(I32, (512, 512), 0) + (m * 512 + 1)
            pick = jnp.where(code_row == wanted, 1.0, 0.0).astype(BF)
            total[m * 512:(m + 1) * 512, :] += jnp.dot(pick, rows, preferred_element_type=F32)
        return carry

    lax.fori_loop(0, 8, compact, 0)
    blocks[0] = total[...].astype(BF)

    def block_copy(src, dst, ch, to):
        rows = pl.ds(ch * CROWS, CROWS)
        return pltpu.make_async_remote_copy(
            src_ref=blocks.at[src, rows], dst_ref=blocks.at[dst, rows],
            send_sem=send_block.at[dst], recv_sem=recv_block.at[dst, ch],
            device_id=to, device_id_type=MESH,
        )

    above = place(x, y, up, core)
    below = place(x, y, down, core)
    beside = place(x, y, z, 1 - core)
    above_beside = place(x, y, up, 1 - core)
    for ch in range(CHUNKS):
        block_copy(0, 1, ch, below).start()
        block_copy(0, 2, ch, above).start()

    def score(row_block, row_at, col_block, col_at):
        rows = jnp.concatenate([blocks[row_block, row_at, :], row_feat[row_block, row_at, :]], axis=1)
        cols = jnp.concatenate([blocks[col_block, col_at, :], col_feat[col_block, col_at, :]], axis=1)
        return lax.dot_general(cols, rows, NT, preferred_element_type=F32)

    def fold(row_block, row_at, scores):
        c, r = scores.shape
        top = jnp.max(scores.reshape(c // 8, 8, r), axis=0)
        best[row_block, :, row_at] = jnp.maximum(best[row_block, :, row_at], top)

    for t in range(8):
        at = pl.ds(t * 256, 256)
        scores = score(0, at, 0, at)
        c = lax.broadcasted_iota(I32, (256, 256), 0)
        r = lax.broadcasted_iota(I32, (256, 256), 1)
        fold(0, at, jnp.where(c < r, scores, -1.0))
        if t:
            fold(0, at, score(0, at, 0, pl.ds(0, t * 256)))

    every = pl.ds(0, ROWS)

    def either(condition, yes, no):
        pl.when(condition)(yes)
        pl.when(jnp.logical_not(condition))(no)

    def meet(row_block, row_at, col_block, col_at):
        fold(row_block, row_at, score(row_block, row_at, col_block, col_at))

    def pair_chunk(p, q, ch):
        at = pl.ds(ch * CROWS, CROWS)
        either(
            numbers[q] > numbers[p],
            lambda: meet(q, at, p, every),
            lambda: meet(p, every, q, at),
        )

    def pair_share(p, q, second, ch):
        at = pl.ds(ch * CROWS, CROWS)
        upto = pl.ds(0, (ch + 1) * CROWS)
        under = pl.ds(0, ch * CROWS)

        def roles(rows, cols):
            def first():
                meet(rows, upto, cols, at)

            def other():
                if ch:
                    meet(rows, at, cols, under)

            either(second == 0, first, other)

        either(numbers[q] > numbers[p], lambda: roles(q, p), lambda: roles(p, q))

    for ch in range(CHUNKS):
        block_copy(0, 1, ch, below).wait_recv()
        block_copy(1, 3, ch, beside).start()
        pair_chunk(0, 1, ch)
        block_copy(0, 2, ch, above).wait_recv()
        pair_share(1, 2, div(z, 2), ch)
        block_copy(1, 3, ch, beside).wait_recv()
        pair_chunk(0, 3, ch)
        pair_share(1, 3, core, ch)
        pair_share(2, 3, 1 - core, ch)

    whole = blocks.at[0]
    for dst in (1, 2, 3):
        part_out[dst] = jnp.max(best[dst], axis=0, keepdims=True)
        pltpu.make_async_remote_copy(
            src_ref=part_out.at[dst], dst_ref=part_in.at[dst], send_sem=send_part.at[dst], recv_sem=recv_part.at[dst],
            device_id=(None, above, below, above_beside)[dst], device_id_type=MESH,
        ).start()
    top = jnp.max(best[0], axis=0, keepdims=True)
    for dst in (1, 2, 3):
        pltpu.make_async_copy(part_in.at[dst], part_in.at[dst], recv_part.at[dst]).wait()
        top = jnp.maximum(top, part_in[dst])

    for k in range(16):
        table[k:k + 1, :] = top[:, k * 128:(k + 1) * 128]
    values = split3(table[...])
    for part in range(4):
        index = jnp.concatenate([codes_of(part * 8 + k) for k in range(8)], axis=1) - 1
        fine = jnp.where((index & 127) == lax.broadcasted_iota(I32, (128, 1024), 0), 1.0, 0.0).astype(BF)
        found = jnp.dot(values, fine, preferred_element_type=F32)
        found = (found[0:16] + found[16:32]) + found[32:48]
        coarse = (index >> 7) == lax.broadcasted_iota(I32, (16, 1024), 0)
        line = jnp.sum(jnp.where(coarse, found, 0.0), axis=0, keepdims=True)
        for k in range(8):
            answer[part * 8 + k] = line[:, k * 128:(k + 1) * 128]

    def send_answer(other, column):
        pltpu.make_async_remote_copy(
            src_ref=answer.at[other * 2 + div(column, 4)], dst_ref=answer_in.at[me], send_sem=send_ans, recv_sem=recv_ans,
            device_id=(other, column), device_id_type=MESH,
        ).start()

    to_all(send_answer)
    pltpu.make_async_copy(answer.at[div(me, 4)], answer_in.at[me], recv_ans).start()
    pltpu.make_async_copy(answer_in, answer_in, recv_ans).wait()

    turned[...] = answer_in[...].reshape(DEV, 128).T
    mine_back = split3(turned[pl.ds(pl.multiple_of(quarter, CAP), CAP), :])
    back = jnp.dot(mine_back, dest_hot[...], preferred_element_type=F32)
    back = (back[0:32] + back[32:64]) + back[64:96]
    spot = pos_row[...] == lax.broadcasted_iota(I32, (CAP, ROWS), 0)
    out_ref[...] = jnp.sum(jnp.where(spot, back, 0.0), axis=0, keepdims=True)

    others = pl.ds(0, DEV - 1)
    pltpu.make_async_copy(slot_in.at[others], slot_in.at[others], send_slot).wait()
    pltpu.make_async_copy(answer_in.at[others], answer_in.at[others], send_ans).wait()
    sent = pl.ds(0, (DEV - 1) * CAP)
    pltpu.make_async_copy(arrived.at[sent], arrived.at[sent], send_row).wait()
    for dst in (1, 2, 3):
        pltpu.make_async_copy(whole, whole, send_block.at[dst]).wait()
        pltpu.make_async_copy(part_in.at[dst], part_in.at[dst], send_part.at[dst]).wait()


def shards(embeddings, cluster_id, member_rank, cluster_size, cluster_owner):
    vmem = pl.BlockSpec(memory_space=pltpu.VMEM)
    dma = pltpu.SemaphoreType.DMA
    result = pl.pallas_call(
        kernel,
        out_shape=jax.ShapeDtypeStruct((1, ROWS), F32),
        in_specs=[pl.BlockSpec(memory_space=pltpu.HBM)] * 5,
        out_specs=vmem,
        scratch_shapes=[
            pltpu.VMEM((ROWS, EMB), BF),
            pltpu.VMEM((1, ROWS), I32),
            pltpu.VMEM((1, ROWS), I32),
            pltpu.SMEM((32,), I32),
            pltpu.SMEM((32,), I32),
            dma((5,)),
            pltpu.VMEM((ROWS, EMB), BF),
            pltpu.VMEM((DEV * CAP, EMB), BF),
            pltpu.VMEM((DEV * CAP, EMB), BF),
            pltpu.VMEM((DEV, 1, 128), I32),
            pltpu.VMEM((DEV, 1, 128), I32),
            pltpu.VMEM((DEV, ROWS), BF),
            pltpu.VMEM((1, ROWS), I32),
            pltpu.VMEM((1, ROWS), I32),
            pltpu.VMEM((1, ROWS), I32),
            pltpu.VMEM((ROWS, EMB), F32),
            pltpu.VMEM((4, ROWS, EMB), BF),
            pltpu.VMEM((4, ROWS, EMB), BF),
            pltpu.VMEM((4, ROWS, EMB), BF),
            pltpu.VMEM((4, 8, ROWS), F32),
            pltpu.VMEM((4, 1, ROWS), F32),
            pltpu.VMEM((4, 1, ROWS), F32),
            pltpu.VMEM((16, 128), F32),
            pltpu.VMEM((32, 1, 128), F32),
            pltpu.VMEM((DEV, 1, 128), F32),
            pltpu.VMEM((128, DEV), F32),
            dma, dma((16,)), dma, dma((16,)), dma((4,)), dma((4, CHUNKS)), dma((4,)), dma((4,)), dma, dma,
        ],
        compiler_params=pltpu.CompilerParams(
            collective_id=0, has_side_effects=True, vmem_limit_bytes=62 * 1024 * 1024
        ),
        cost_estimate=pl.CostEstimate(flops=12 * 10**9, bytes_accessed=1 << 20, transcendentals=2048),
    )(embeddings, cluster_id.reshape(1, ROWS), member_rank.reshape(1, ROWS), cluster_size, cluster_owner)
    return result.reshape(ROWS)


def solution(mesh):
    in_specs = (P(("dp", "narrow"), None), P(("dp", "narrow")), P(("dp", "narrow")), P(), P())
    out_specs = P(("dp", "narrow"))
    return jax.shard_map(shards, mesh=mesh, in_specs=in_specs, out_specs=out_specs, check_vma=False)
```

```python
import jax
import jax.numpy as jnp
from jax import lax
from jax.experimental import pallas as pl
from jax.experimental.pallas import tpu as pltpu
from jax.sharding import PartitionSpec as P

MESH = pl.DeviceIdType.MESH
NT = (((1,), (1,)), ((), ()))
DEV = 128
CAP = 32
ROWS = 2048
EMB = 128
EDGES = (0, 512, 1024, 1536, 2048)
CHUNKS = len(EDGES) - 1
BF = jnp.bfloat16
F32 = jnp.float32
I32 = jnp.int32


def div(a, b):
    return lax.div(a, jnp.int32(b))


def rem(a, b):
    return lax.rem(a, jnp.int32(b))


def place(x, y, z, core):
    return (y * 4 + rem(x, 2) * 2 + core, z * 2 + div(x, 2))


def split3(value):
    high = value.astype(BF)
    rest = value - high.astype(F32)
    middle = rest.astype(BF)
    low = (rest - middle.astype(F32)).astype(BF)
    return jnp.concatenate([high, middle, low], axis=0)


def kernel(
    emb_hbm, cid_hbm, rank_hbm, size_hbm, owner_hbm, out_ref,
    emb_ref, cid_ref, rank_ref, size_ref, owner_ref, load_sem,
    normed, bucket, arrived, slot_out, slot_in, dest_hot, dest_row, pos_row, flat_row,
    total, blocks, row_feat, col_feat, best, part_out, part_in, table, fine, coarse, answer, answer_in, turned,
    send_slot, recv_slot, send_row, recv_row, send_block, recv_block, send_part, recv_part, send_ans, recv_ans,
):
    dp = lax.axis_index("dp")
    nar = lax.axis_index("narrow")
    y, core = div(dp, 4), rem(dp, 2)
    x = rem(nar, 2) * 2 + rem(div(dp, 2), 2)
    z = div(nar, 2)
    group = y * 4 + x
    member = z * 2 + core
    me = dp * 8 + nar
    quarter = rem(me, 4) * CAP

    loads = [
        pltpu.make_async_copy(src, dst, load_sem.at[k])
        for k, (src, dst) in enumerate(
            ((owner_hbm, owner_ref), (size_hbm, size_ref), (cid_hbm, cid_ref), (rank_hbm, rank_ref), (emb_hbm, emb_ref))
        )
    ]
    for load in loads:
        load.start()

    barrier = pltpu.get_barrier_semaphore()

    def to_all(act):
        def line(i, carry):
            other = rem(dp + i, 16)
            for j in range(8):
                act(other, rem(nar + j, 8))
            return carry

        lax.fori_loop(1, 16, line, 0)
        for j in range(1, 8):
            act(dp, rem(nar + j, 8))

    def greet(other, column):
        pl.semaphore_signal(barrier, inc=1, device_id=(other, column), device_id_type=MESH)

    to_all(greet)
    for load in loads:
        load.wait()

    cid = cid_ref[...]

    def owners(j, carry):
        owner, bound, seen = carry
        own = owner_ref[j]
        owner = jnp.where(cid == j, own, owner)
        mine = own == group
        bound = jnp.where(mine & (seen == 0), size_ref[j], bound)
        seen = jnp.where(mine, 1, seen)
        return owner, bound, seen

    owner, bound, _ = lax.fori_loop(
        0, 32, owners, (jnp.zeros((1, ROWS), I32), jnp.int32(0), jnp.int32(0))
    )

    def offsets(j, offset):
        return offset + jnp.where((owner == owner_ref[j]) & (cid > j), size_ref[j], 0)

    offset = lax.fori_loop(0, 32, offsets, rank_ref[...])
    seat = offset >> 11
    dest = (
        ((owner >> 2) << 5) + ((owner & 1) << 4) + ((seat & 1) << 3) + ((seat >> 1) << 1) + ((owner >> 1) & 1)
    )
    local = offset & (ROWS - 1)
    dest_row[...] = dest

    hot = dest == lax.broadcasted_iota(I32, (DEV, ROWS), 0)
    dest_hot[...] = jnp.where(hot, 1.0, 0.0).astype(BF)
    upper = jnp.where(
        lax.broadcasted_iota(I32, (256, 256), 0) <= lax.broadcasted_iota(I32, (256, 256), 1), 1.0, 0.0
    ).astype(BF)
    before = jnp.full((DEV, 1), -1.0, F32)
    for k in range(ROWS // 256):
        piece = dest_hot[:, k * 256:(k + 1) * 256]
        count = jnp.dot(piece, upper, preferred_element_type=F32)
        position = jnp.sum(jnp.where(piece.astype(F32) > 0.5, count + before, 0.0), axis=0, keepdims=True)
        pos_row[:, k * 256:(k + 1) * 256] = position.astype(I32)
        before = before + count[:, 255:256]
    pos = pos_row[...]
    flat_row[...] = dest * CAP + pos

    lane_hot = (pos + quarter) == lax.broadcasted_iota(I32, (DEV, ROWS), 0)
    code = local + 1
    high = jnp.where(lane_hot, (code & ~63).astype(F32), 0.0).astype(BF)
    low = jnp.where(lane_hot, (code & 63).astype(F32), 0.0).astype(BF)
    codes = lax.dot_general(dest_hot[...], high, NT, preferred_element_type=F32)
    codes = codes + lax.dot_general(dest_hot[...], low, NT, preferred_element_type=F32)
    slot_out[...] = codes.astype(I32).reshape(DEV, 1, 128)

    wide = emb_ref[...].astype(F32)
    normed[...] = (wide * lax.rsqrt(jnp.sum(wide * wide, axis=1, keepdims=True) + 1e-06)).astype(BF)

    pl.semaphore_wait(barrier, DEV - 1)

    total[...] = jnp.zeros((ROWS, EMB), F32)
    def hot_rows(number, size):
        number = jnp.where((number >= 0) & (number < size), number, -1).astype(F32).astype(BF)
        count = lax.broadcasted_iota(I32, (size, number.shape[1]), 0).astype(F32).astype(BF)
        return jnp.where(number == count, jnp.ones((), BF), jnp.zeros((), BF))

    def fill(other):
        pick = hot_rows(flat_row[...] - other * 256, 256)
        rows = jnp.dot(pick, normed[...], preferred_element_type=F32)
        bucket[pl.ds(pl.multiple_of(other * 256, 256), 256), :] = rows.astype(BF)

    def send_rows(other, j):
        column = rem(nar + 3 * j % 8, 8)
        to = other * 8 + column
        pltpu.make_async_remote_copy(
            src_ref=slot_out.at[to], dst_ref=slot_in.at[me], send_sem=send_slot, recv_sem=recv_slot.at[dp],
            device_id=(other, column), device_id_type=MESH,
        ).start()
        pltpu.make_async_remote_copy(
            src_ref=bucket.at[pl.ds(pl.multiple_of(to * CAP, CAP), CAP)],
            dst_ref=arrived.at[pl.ds(pl.multiple_of(me * CAP, CAP), CAP)],
            send_sem=send_row, recv_sem=recv_row.at[dp],
            device_id=(other, column), device_id_type=MESH,
        ).start()

    def dispatch(i, carry):
        other = rem(dp + 5 * i, 16)
        fill(other)
        for j in range(8):
            send_rows(other, j)
        return carry


    def codes_of(k):
        return jnp.sum(slot_in[pl.ds(4 * k, 4)], axis=0)

    def gather_in(i):
        rows, codes = [], []
        for k in range(2):
            other = rem(dp + 80 - 5 * (2 * i + 1 + k), 16)
            at = pl.ds(pl.multiple_of(other * 256, 256), 256)
            ats = pl.ds(pl.multiple_of(other * 8, 8), 8)
            pltpu.make_async_copy(slot_in.at[ats], slot_in.at[ats], recv_slot.at[other]).wait()
            pltpu.make_async_copy(arrived.at[at], arrived.at[at], recv_row.at[other]).wait()
            codes += [codes_of(2 * other), codes_of(2 * other + 1)]
            rows.append(arrived[at, :])
        return jnp.concatenate(codes, axis=1), jnp.concatenate(rows, axis=0)

    def placed(ch, code_row, rows):
        low, high = EDGES[ch], EDGES[ch + 1]
        pick = jnp.concatenate([hot_rows(code_row - (first + 1), 256) for first in range(low, high, 256)], axis=0)
        return total[low:high, :] + jnp.dot(pick, rows, preferred_element_type=F32)

    def compact(i, carry):
        code_row, rows = gather_in(i)
        for ch in range(CHUNKS):
            total[EDGES[ch]:EDGES[ch + 1], :] = placed(ch, code_row, rows)
        return carry

    def dispatch_own():
        fill(dp)
        for j in range(1, 8):
            send_rows(dp, j)
        mine = pl.ds(pl.multiple_of(me * CAP, CAP), CAP)
        pltpu.make_async_copy(slot_out.at[me], slot_in.at[me], recv_slot.at[dp]).start()
        pltpu.make_async_copy(bucket.at[mine], arrived.at[mine], recv_row.at[dp]).start()

    lax.fori_loop(1, 16, dispatch, 0)
    dispatch_own()
    lax.fori_loop(0, 7, compact, 0)

    def span(ch):
        return pl.ds(EDGES[ch], EDGES[ch + 1] - EDGES[ch])

    def block_copy(src, dst, ch, to):
        rows = span(ch)
        return pltpu.make_async_remote_copy(
            src_ref=blocks.at[src, rows], dst_ref=blocks.at[dst, rows],
            send_sem=send_block.at[dst], recv_sem=recv_block.at[dst, ch],
            device_id=to, device_id_type=MESH,
        )

    up = rem(z + 1, 4)
    down = rem(z + 3, 4)
    above = place(x, y, up, core)
    below = place(x, y, down, core)
    beside = place(x, y, z, 1 - core)
    above_beside = place(x, y, up, 1 - core)
    code_row, rows = gather_in(7)
    for ch in range(CHUNKS):
        blocks[0, EDGES[ch]:EDGES[ch + 1], :] = placed(ch, code_row, rows).astype(BF)
        block_copy(0, 1, ch, below).start()
        block_copy(0, 2, ch, above).start()

    first_lane = lax.broadcasted_iota(I32, (256, EMB), 1) == 0
    numbers = (member, up * 2 + core, down * 2 + core, up * 2 + 1 - core)
    for b in range(4):
        def features(t, carry):
            at = pl.ds(pl.multiple_of(t * 256, 256), 256)
            slot = numbers[b] * ROWS + t * 256 + lax.broadcasted_iota(I32, (256, EMB), 0)
            late = slot >= bound
            row_feat[b, at, :] = jnp.where(first_lane & late, 1.0, 0.0).astype(BF)
            col_feat[b, at, :] = jnp.where(first_lane & jnp.logical_not(late), -8.0, 0.0).astype(BF)
            return carry

        lax.fori_loop(0, 8, features, 0)
    best[...] = jnp.full((4, 8, ROWS), -1.0, F32)

    for part in range(4):
        index = jnp.concatenate([codes_of(part * 8 + k) for k in range(8)], axis=1) - 1
        at = pl.ds(part * 1024, 1024)
        fine[:, at] = jnp.where((index & 127) == lax.broadcasted_iota(I32, (128, 1024), 0), 1.0, 0.0).astype(BF)
        coarse[:, at] = jnp.where((index >> 7) == lax.broadcasted_iota(I32, (16, 1024), 0), 1.0, 0.0)

    def score(row_block, row_at, col_block, col_at):
        rows = jnp.concatenate([blocks[row_block, row_at, :], row_feat[row_block, row_at, :]], axis=1)
        cols = jnp.concatenate([blocks[col_block, col_at, :], col_feat[col_block, col_at, :]], axis=1)
        return lax.dot_general(cols, rows, NT, preferred_element_type=F32)

    def fold(row_block, row_at, scores):
        c, r = scores.shape
        top = jnp.max(scores.reshape(c // 8, 8, r), axis=0)
        best[row_block, :, row_at] = jnp.maximum(best[row_block, :, row_at], top)

    for t in range(8):
        at = pl.ds(t * 256, 256)
        scores = score(0, at, 0, at)
        c = lax.broadcasted_iota(I32, (256, 256), 0)
        r = lax.broadcasted_iota(I32, (256, 256), 1)
        fold(0, at, jnp.where(c < r, scores, -1.0))
        if t:
            fold(0, at, score(0, at, 0, pl.ds(0, t * 256)))

    every = pl.ds(0, ROWS)

    def either(condition, yes, no):
        pl.when(condition)(yes)
        pl.when(jnp.logical_not(condition))(no)

    def meet(row_block, row_at, col_block, col_at):
        fold(row_block, row_at, score(row_block, row_at, col_block, col_at))

    def pair_chunk(p, q, ch):
        at = span(ch)
        either(
            numbers[q] > numbers[p],
            lambda: meet(q, at, p, every),
            lambda: meet(p, every, q, at),
        )

    def pair_share(p, q, second, ch):
        at = span(ch)
        upto = pl.ds(0, EDGES[ch + 1])
        under = pl.ds(0, EDGES[ch])

        def roles(rows, cols):
            def first():
                meet(rows, upto, cols, at)

            def other():
                if ch:
                    meet(rows, at, cols, under)

            either(second == 0, first, other)

        either(numbers[q] > numbers[p], lambda: roles(q, p), lambda: roles(p, q))

    for ch in range(CHUNKS):
        block_copy(0, 1, ch, below).wait_recv()
        block_copy(1, 3, ch, beside).start()
        pair_chunk(0, 1, ch)
        block_copy(0, 2, ch, above).wait_recv()
        pair_share(1, 2, div(z, 2), ch)
        block_copy(1, 3, ch, beside).wait_recv()
        pair_chunk(0, 3, ch)
        pair_share(1, 3, core, ch)
        pair_share(2, 3, 1 - core, ch)

    whole = blocks.at[0]
    for dst in (1, 2, 3):
        part_out[dst] = jnp.max(best[dst], axis=0, keepdims=True)
        pltpu.make_async_remote_copy(
            src_ref=part_out.at[dst], dst_ref=part_in.at[dst], send_sem=send_part.at[dst], recv_sem=recv_part.at[dst],
            device_id=(None, above, below, above_beside)[dst], device_id_type=MESH,
        ).start()
    top = jnp.max(best[0], axis=0, keepdims=True)
    for dst in (1, 2, 3):
        pltpu.make_async_copy(part_in.at[dst], part_in.at[dst], recv_part.at[dst]).wait()
        top = jnp.maximum(top, part_in[dst])

    for k in range(16):
        table[k:k + 1, :] = top[:, k * 128:(k + 1) * 128]
    values = split3(table[...])
    found = jnp.dot(values, fine[...], preferred_element_type=F32)
    found = (found[0:16] + found[16:32]) + found[32:48]
    line = jnp.sum(jnp.where(coarse[...] > 0.5, found, 0.0), axis=0, keepdims=True)
    for k in range(32):
        answer[k] = line[:, k * 128:(k + 1) * 128]

    def send_answer(other, column):
        pltpu.make_async_remote_copy(
            src_ref=answer.at[other * 2 + div(column, 4)], dst_ref=answer_in.at[me], send_sem=send_ans, recv_sem=recv_ans,
            device_id=(other, column), device_id_type=MESH,
        ).start()

    to_all(send_answer)
    pltpu.make_async_copy(answer.at[div(me, 4)], answer_in.at[me], recv_ans).start()
    pltpu.make_async_copy(answer_in, answer_in, recv_ans).wait()

    turned[...] = answer_in[...].reshape(DEV, 128).T
    mine_back = split3(turned[pl.ds(pl.multiple_of(quarter, CAP), CAP), :])
    back = jnp.dot(mine_back, dest_hot[...], preferred_element_type=F32)
    back = (back[0:32] + back[32:64]) + back[64:96]
    spot = pos_row[...] == lax.broadcasted_iota(I32, (CAP, ROWS), 0)
    out_ref[...] = jnp.sum(jnp.where(spot, back, 0.0), axis=0, keepdims=True)

    others = pl.ds(0, DEV - 1)
    pltpu.make_async_copy(slot_in.at[others], slot_in.at[others], send_slot).wait()
    pltpu.make_async_copy(answer_in.at[others], answer_in.at[others], send_ans).wait()
    sent = pl.ds(0, (DEV - 1) * CAP)
    pltpu.make_async_copy(arrived.at[sent], arrived.at[sent], send_row).wait()
    for dst in (1, 2, 3):
        pltpu.make_async_copy(whole, whole, send_block.at[dst]).wait()
        pltpu.make_async_copy(part_in.at[dst], part_in.at[dst], send_part.at[dst]).wait()


def shards(embeddings, cluster_id, member_rank, cluster_size, cluster_owner):
    vmem = pl.BlockSpec(memory_space=pltpu.VMEM)
    dma = pltpu.SemaphoreType.DMA
    result = pl.pallas_call(
        kernel,
        out_shape=jax.ShapeDtypeStruct((1, ROWS), F32),
        in_specs=[pl.BlockSpec(memory_space=pltpu.HBM)] * 5,
        out_specs=vmem,
        scratch_shapes=[
            pltpu.VMEM((ROWS, EMB), BF),
            pltpu.VMEM((1, ROWS), I32),
            pltpu.VMEM((1, ROWS), I32),
            pltpu.SMEM((32,), I32),
            pltpu.SMEM((32,), I32),
            dma((5,)),
            pltpu.VMEM((ROWS, EMB), BF),
            pltpu.VMEM((DEV * CAP, EMB), BF),
            pltpu.VMEM((DEV * CAP, EMB), BF),
            pltpu.VMEM((DEV, 1, 128), I32),
            pltpu.VMEM((DEV, 1, 128), I32),
            pltpu.VMEM((DEV, ROWS), BF),
            pltpu.VMEM((1, ROWS), I32),
            pltpu.VMEM((1, ROWS), I32),
            pltpu.VMEM((1, ROWS), I32),
            pltpu.VMEM((ROWS, EMB), F32),
            pltpu.VMEM((4, ROWS, EMB), BF),
            pltpu.VMEM((4, ROWS, EMB), BF),
            pltpu.VMEM((4, ROWS, EMB), BF),
            pltpu.VMEM((4, 8, ROWS), F32),
            pltpu.VMEM((4, 1, ROWS), F32),
            pltpu.VMEM((4, 1, ROWS), F32),
            pltpu.VMEM((16, 128), F32),
            pltpu.VMEM((128, DEV * CAP), BF),
            pltpu.VMEM((16, DEV * CAP), F32),
            pltpu.VMEM((32, 1, 128), F32),
            pltpu.VMEM((DEV, 1, 128), F32),
            pltpu.VMEM((128, DEV), F32),
            dma, dma((16,)), dma, dma((16,)), dma((4,)), dma((4, CHUNKS)), dma((4,)), dma((4,)), dma, dma,
        ],
        compiler_params=pltpu.CompilerParams(
            collective_id=0, has_side_effects=True, vmem_limit_bytes=62 * 1024 * 1024
        ),
        cost_estimate=pl.CostEstimate(flops=12 * 10**9, bytes_accessed=1 << 20, transcendentals=2048),
    )(embeddings, cluster_id.reshape(1, ROWS), member_rank.reshape(1, ROWS), cluster_size, cluster_owner)
    return result.reshape(ROWS)


def solution(mesh):
    in_specs = (P(("dp", "narrow"), None), P(("dp", "narrow")), P(("dp", "narrow")), P(), P())
    out_specs = P(("dp", "narrow"))
    return jax.shard_map(shards, mesh=mesh, in_specs=in_specs, out_specs=out_specs, check_vma=False)
```

```python
import jax
import jax.numpy as jnp
from jax import lax
from jax.experimental import pallas as pl
from jax.experimental.pallas import tpu as pltpu
from jax.sharding import PartitionSpec as P

MESH = pl.DeviceIdType.MESH
NT = (((1,), (1,)), ((), ()))
DEV = 128
CAP = 32
ROWS = 2048
EMB = 128
EDGES = (0, 512, 1024, 1536, 2048)
CHUNKS = len(EDGES) - 1
BF = jnp.bfloat16
F32 = jnp.float32
I32 = jnp.int32


def div(a, b):
    return lax.div(a, jnp.int32(b))


def rem(a, b):
    return lax.rem(a, jnp.int32(b))


def place(x, y, z, core):
    return (y * 4 + rem(x, 2) * 2 + core, z * 2 + div(x, 2))


def split3(value):
    high = value.astype(BF)
    rest = value - high.astype(F32)
    middle = rest.astype(BF)
    low = (rest - middle.astype(F32)).astype(BF)
    return jnp.concatenate([high, middle, low], axis=0)


def kernel(
    emb_hbm, cid_hbm, rank_hbm, size_hbm, owner_hbm, out_ref,
    emb_ref, cid_ref, rank_ref, size_ref, owner_ref, load_sem,
    normed, bucket, arrived, slot_out, slot_in, dest_hot, dest_row, pos_row, flat_row,
    total, blocks, row_feat, col_feat, best, part_out, part_in, table, fine, coarse, answer, answer_in, turned,
    send_slot, recv_slot, send_row, recv_row, send_block, recv_block, send_part, recv_part, send_ans, recv_ans,
):
    dp = lax.axis_index("dp")
    nar = lax.axis_index("narrow")
    y, core = div(dp, 4), rem(dp, 2)
    x = rem(nar, 2) * 2 + rem(div(dp, 2), 2)
    z = div(nar, 2)
    group = y * 4 + x
    member = z * 2 + core
    me = dp * 8 + nar
    quarter = rem(me, 4) * CAP

    loads = [
        pltpu.make_async_copy(src, dst, load_sem.at[k])
        for k, (src, dst) in enumerate(
            ((owner_hbm, owner_ref), (size_hbm, size_ref), (cid_hbm, cid_ref), (rank_hbm, rank_ref), (emb_hbm, emb_ref))
        )
    ]
    for load in loads:
        load.start()

    barrier = pltpu.get_barrier_semaphore()

    def to_all(act, stride=1):
        def line(i, carry):
            other = rem(dp + stride * i, 16)
            for j in range(8):
                act(other, rem(nar + j, 8))
            return carry

        lax.fori_loop(1, 16, line, 0)
        for j in range(1, 8):
            act(dp, rem(nar + j, 8))

    def greet(other, column):
        pl.semaphore_signal(barrier, inc=1, device_id=(other, column), device_id_type=MESH)

    to_all(greet)
    for load in loads:
        load.wait()

    cid = cid_ref[...]

    def owners(j, carry):
        owner, bound, seen = carry
        own = owner_ref[j]
        owner = jnp.where(cid == j, own, owner)
        mine = own == group
        bound = jnp.where(mine & (seen == 0), size_ref[j], bound)
        seen = jnp.where(mine, 1, seen)
        return owner, bound, seen

    owner, bound, _ = lax.fori_loop(
        0, 32, owners, (jnp.zeros((1, ROWS), I32), jnp.int32(0), jnp.int32(0))
    )

    def offsets(j, offset):
        return offset + jnp.where((owner == owner_ref[j]) & (cid > j), size_ref[j], 0)

    offset = lax.fori_loop(0, 32, offsets, rank_ref[...])
    seat = offset >> 11
    dest = (
        ((owner >> 2) << 5) + ((owner & 1) << 4) + ((seat & 1) << 3) + ((seat >> 1) << 1) + ((owner >> 1) & 1)
    )
    local = offset & (ROWS - 1)
    dest_row[...] = dest

    hot = dest == lax.broadcasted_iota(I32, (DEV, ROWS), 0)
    dest_hot[...] = jnp.where(hot, 1.0, 0.0).astype(BF)
    upper = jnp.where(
        lax.broadcasted_iota(I32, (256, 256), 0) <= lax.broadcasted_iota(I32, (256, 256), 1), 1.0, 0.0
    ).astype(BF)
    before = jnp.full((DEV, 1), -1.0, F32)
    for k in range(ROWS // 256):
        piece = dest_hot[:, k * 256:(k + 1) * 256]
        count = jnp.dot(piece, upper, preferred_element_type=F32)
        position = jnp.sum(jnp.where(piece.astype(F32) > 0.5, count + before, 0.0), axis=0, keepdims=True)
        pos_row[:, k * 256:(k + 1) * 256] = position.astype(I32)
        before = before + count[:, 255:256]
    pos = pos_row[...]
    flat_row[...] = dest * CAP + pos

    lane_hot = (pos + quarter) == lax.broadcasted_iota(I32, (DEV, ROWS), 0)
    code = local + 1
    high = jnp.where(lane_hot, (code & ~63).astype(F32), 0.0).astype(BF)
    low = jnp.where(lane_hot, (code & 63).astype(F32), 0.0).astype(BF)
    codes = lax.dot_general(dest_hot[...], high, NT, preferred_element_type=F32)
    codes = codes + lax.dot_general(dest_hot[...], low, NT, preferred_element_type=F32)
    slot_out[...] = codes.astype(I32).reshape(DEV, 1, 128)

    wide = emb_ref[...].astype(F32)
    normed[...] = (wide * lax.rsqrt(jnp.sum(wide * wide, axis=1, keepdims=True) + 1e-06)).astype(BF)

    pl.semaphore_wait(barrier, DEV - 1)

    total[...] = jnp.zeros((ROWS, EMB), F32)
    def hot_rows(number, size):
        number = jnp.where((number >= 0) & (number < size), number, -1).astype(F32).astype(BF)
        count = lax.broadcasted_iota(I32, (size, number.shape[1]), 0).astype(F32).astype(BF)
        return jnp.where(number == count, jnp.ones((), BF), jnp.zeros((), BF))

    def fill(other):
        pick = hot_rows(flat_row[...] - other * 256, 256)
        rows = jnp.dot(pick, normed[...], preferred_element_type=F32)
        bucket[pl.ds(pl.multiple_of(other * 256, 256), 256), :] = rows.astype(BF)

    def send_rows(other, j):
        column = rem(nar + 3 * j % 8, 8)
        to = other * 8 + column
        pltpu.make_async_remote_copy(
            src_ref=slot_out.at[to], dst_ref=slot_in.at[me], send_sem=send_slot, recv_sem=recv_slot.at[dp],
            device_id=(other, column), device_id_type=MESH,
        ).start()
        pltpu.make_async_remote_copy(
            src_ref=bucket.at[pl.ds(pl.multiple_of(to * CAP, CAP), CAP)],
            dst_ref=arrived.at[pl.ds(pl.multiple_of(me * CAP, CAP), CAP)],
            send_sem=send_row, recv_sem=recv_row.at[dp],
            device_id=(other, column), device_id_type=MESH,
        ).start()

    def dispatch(i, carry):
        other = rem(dp + 5 * i, 16)
        fill(other)
        for j in range(8):
            send_rows(other, j)
        return carry


    def codes_of(k):
        return jnp.sum(slot_in[pl.ds(4 * k, 4)], axis=0)

    def gather_in(i):
        rows, codes = [], []
        for k in range(2):
            other = rem(dp + 80 - 5 * (2 * i + 1 + k), 16)
            at = pl.ds(pl.multiple_of(other * 256, 256), 256)
            ats = pl.ds(pl.multiple_of(other * 8, 8), 8)
            pltpu.make_async_copy(slot_in.at[ats], slot_in.at[ats], recv_slot.at[other]).wait()
            pltpu.make_async_copy(arrived.at[at], arrived.at[at], recv_row.at[other]).wait()
            codes += [codes_of(2 * other), codes_of(2 * other + 1)]
            rows.append(arrived[at, :])
        return jnp.concatenate(codes, axis=1), jnp.concatenate(rows, axis=0)

    def placed(ch, code_row, rows):
        low, high = EDGES[ch], EDGES[ch + 1]
        pick = jnp.concatenate([hot_rows(code_row - (first + 1), 256) for first in range(low, high, 256)], axis=0)
        return total[low:high, :] + jnp.dot(pick, rows, preferred_element_type=F32)

    def compact(i, carry):
        code_row, rows = gather_in(i)
        for ch in range(CHUNKS):
            total[EDGES[ch]:EDGES[ch + 1], :] = placed(ch, code_row, rows)
        return carry

    def dispatch_own():
        fill(dp)
        for j in range(1, 8):
            send_rows(dp, j)
        mine = pl.ds(pl.multiple_of(me * CAP, CAP), CAP)
        pltpu.make_async_copy(slot_out.at[me], slot_in.at[me], recv_slot.at[dp]).start()
        pltpu.make_async_copy(bucket.at[mine], arrived.at[mine], recv_row.at[dp]).start()

    lax.fori_loop(1, 16, dispatch, 0)
    dispatch_own()
    lax.fori_loop(0, 7, compact, 0)

    def span(ch):
        return pl.ds(EDGES[ch], EDGES[ch + 1] - EDGES[ch])

    def block_copy(src, dst, ch, to):
        rows = span(ch)
        return pltpu.make_async_remote_copy(
            src_ref=blocks.at[src, rows], dst_ref=blocks.at[dst, rows],
            send_sem=send_block.at[dst], recv_sem=recv_block.at[dst, ch],
            device_id=to, device_id_type=MESH,
        )

    up = rem(z + 1, 4)
    down = rem(z + 3, 4)
    above = place(x, y, up, core)
    below = place(x, y, down, core)
    beside = place(x, y, z, 1 - core)
    above_beside = place(x, y, up, 1 - core)
    code_row, rows = gather_in(7)
    for ch in range(CHUNKS):
        blocks[0, EDGES[ch]:EDGES[ch + 1], :] = placed(ch, code_row, rows).astype(BF)
        block_copy(0, 1, ch, below).start()
        block_copy(0, 2, ch, above).start()

    first_lane = lax.broadcasted_iota(I32, (256, EMB), 1) == 0
    numbers = (member, up * 2 + core, down * 2 + core, up * 2 + 1 - core)
    for b in range(4):
        def features(t, carry):
            at = pl.ds(pl.multiple_of(t * 256, 256), 256)
            slot = numbers[b] * ROWS + t * 256 + lax.broadcasted_iota(I32, (256, EMB), 0)
            late = slot >= bound
            row_feat[b, at, :] = jnp.where(first_lane & late, 1.0, 0.0).astype(BF)
            col_feat[b, at, :] = jnp.where(first_lane & jnp.logical_not(late), -8.0, 0.0).astype(BF)
            return carry

        lax.fori_loop(0, 8, features, 0)
    best[...] = jnp.full((4, 8, ROWS), -1.0, F32)

    for part in range(4):
        index = jnp.concatenate([codes_of(part * 8 + k) for k in range(8)], axis=1) - 1
        at = pl.ds(part * 1024, 1024)
        fine[:, at] = jnp.where((index & 127) == lax.broadcasted_iota(I32, (128, 1024), 0), 1.0, 0.0).astype(BF)
        coarse[:, at] = jnp.where((index >> 7) == lax.broadcasted_iota(I32, (16, 1024), 0), 1.0, 0.0)

    def score(row_block, row_at, col_block, col_at):
        rows = jnp.concatenate([blocks[row_block, row_at, :], row_feat[row_block, row_at, :]], axis=1)
        cols = jnp.concatenate([blocks[col_block, col_at, :], col_feat[col_block, col_at, :]], axis=1)
        return lax.dot_general(cols, rows, NT, preferred_element_type=F32)

    def fold(row_block, row_at, scores):
        c, r = scores.shape
        top = jnp.max(scores.reshape(c // 8, 8, r), axis=0)
        best[row_block, :, row_at] = jnp.maximum(best[row_block, :, row_at], top)

    for t in range(8):
        at = pl.ds(t * 256, 256)
        scores = score(0, at, 0, at)
        c = lax.broadcasted_iota(I32, (256, 256), 0)
        r = lax.broadcasted_iota(I32, (256, 256), 1)
        fold(0, at, jnp.where(c < r, scores, -1.0))
        if t:
            fold(0, at, score(0, at, 0, pl.ds(0, t * 256)))

    every = pl.ds(0, ROWS)

    def either(condition, yes, no):
        pl.when(condition)(yes)
        pl.when(jnp.logical_not(condition))(no)

    def meet(row_block, row_at, col_block, col_at):
        fold(row_block, row_at, score(row_block, row_at, col_block, col_at))

    def pair_chunk(p, q, ch):
        at = span(ch)
        either(
            numbers[q] > numbers[p],
            lambda: meet(q, at, p, every),
            lambda: meet(p, every, q, at),
        )

    def pair_share(p, q, second, ch):
        at = span(ch)
        upto = pl.ds(0, EDGES[ch + 1])
        under = pl.ds(0, EDGES[ch])

        def roles(rows, cols):
            def first():
                meet(rows, upto, cols, at)

            def other():
                if ch:
                    meet(rows, at, cols, under)

            either(second == 0, first, other)

        either(numbers[q] > numbers[p], lambda: roles(q, p), lambda: roles(p, q))

    for ch in range(CHUNKS):
        block_copy(0, 1, ch, below).wait_recv()
        block_copy(1, 3, ch, beside).start()
        pair_chunk(0, 1, ch)
        block_copy(0, 2, ch, above).wait_recv()
        pair_share(1, 2, div(z, 2), ch)
        block_copy(1, 3, ch, beside).wait_recv()
        pair_chunk(0, 3, ch)
        pair_share(1, 3, core, ch)
        pair_share(2, 3, 1 - core, ch)

    whole = blocks.at[0]
    for dst in (1, 2, 3):
        part_out[dst] = jnp.max(best[dst], axis=0, keepdims=True)
        pltpu.make_async_remote_copy(
            src_ref=part_out.at[dst], dst_ref=part_in.at[dst], send_sem=send_part.at[dst], recv_sem=recv_part.at[dst],
            device_id=(None, above, below, above_beside)[dst], device_id_type=MESH,
        ).start()
    top = jnp.max(best[0], axis=0, keepdims=True)
    for dst in (1, 2, 3):
        pltpu.make_async_copy(part_in.at[dst], part_in.at[dst], recv_part.at[dst]).wait()
        top = jnp.maximum(top, part_in[dst])

    for k in range(16):
        table[k:k + 1, :] = top[:, k * 128:(k + 1) * 128]
    values = split3(table[...])
    found = jnp.dot(values, fine[...], preferred_element_type=F32)
    found = (found[0:16] + found[16:32]) + found[32:48]
    line = jnp.sum(jnp.where(coarse[...] > 0.5, found, 0.0), axis=0, keepdims=True)
    for k in range(32):
        answer[k] = line[:, k * 128:(k + 1) * 128]

    def send_answer(other, column):
        pltpu.make_async_remote_copy(
            src_ref=answer.at[other * 2 + div(column, 4)], dst_ref=answer_in.at[me], send_sem=send_ans, recv_sem=recv_ans,
            device_id=(other, column), device_id_type=MESH,
        ).start()

    to_all(send_answer, 5)
    pltpu.make_async_copy(answer.at[div(me, 4)], answer_in.at[me], recv_ans).start()
    pltpu.make_async_copy(answer_in, answer_in, recv_ans).wait()

    turned[...] = answer_in[...].reshape(DEV, 128).T
    mine_back = split3(turned[pl.ds(pl.multiple_of(quarter, CAP), CAP), :])
    back = jnp.dot(mine_back, dest_hot[...], preferred_element_type=F32)
    back = (back[0:32] + back[32:64]) + back[64:96]
    spot = pos_row[...] == lax.broadcasted_iota(I32, (CAP, ROWS), 0)
    out_ref[...] = jnp.sum(jnp.where(spot, back, 0.0), axis=0, keepdims=True)

    others = pl.ds(0, DEV - 1)
    pltpu.make_async_copy(slot_in.at[others], slot_in.at[others], send_slot).wait()
    pltpu.make_async_copy(answer_in.at[others], answer_in.at[others], send_ans).wait()
    sent = pl.ds(0, (DEV - 1) * CAP)
    pltpu.make_async_copy(arrived.at[sent], arrived.at[sent], send_row).wait()
    for dst in (1, 2, 3):
        pltpu.make_async_copy(whole, whole, send_block.at[dst]).wait()
        pltpu.make_async_copy(part_in.at[dst], part_in.at[dst], send_part.at[dst]).wait()


def shards(embeddings, cluster_id, member_rank, cluster_size, cluster_owner):
    vmem = pl.BlockSpec(memory_space=pltpu.VMEM)
    dma = pltpu.SemaphoreType.DMA
    result = pl.pallas_call(
        kernel,
        out_shape=jax.ShapeDtypeStruct((1, ROWS), F32),
        in_specs=[pl.BlockSpec(memory_space=pltpu.HBM)] * 5,
        out_specs=vmem,
        scratch_shapes=[
            pltpu.VMEM((ROWS, EMB), BF),
            pltpu.VMEM((1, ROWS), I32),
            pltpu.VMEM((1, ROWS), I32),
            pltpu.SMEM((32,), I32),
            pltpu.SMEM((32,), I32),
            dma((5,)),
            pltpu.VMEM((ROWS, EMB), BF),
            pltpu.VMEM((DEV * CAP, EMB), BF),
            pltpu.VMEM((DEV * CAP, EMB), BF),
            pltpu.VMEM((DEV, 1, 128), I32),
            pltpu.VMEM((DEV, 1, 128), I32),
            pltpu.VMEM((DEV, ROWS), BF),
            pltpu.VMEM((1, ROWS), I32),
            pltpu.VMEM((1, ROWS), I32),
            pltpu.VMEM((1, ROWS), I32),
            pltpu.VMEM((ROWS, EMB), F32),
            pltpu.VMEM((4, ROWS, EMB), BF),
            pltpu.VMEM((4, ROWS, EMB), BF),
            pltpu.VMEM((4, ROWS, EMB), BF),
            pltpu.VMEM((4, 8, ROWS), F32),
            pltpu.VMEM((4, 1, ROWS), F32),
            pltpu.VMEM((4, 1, ROWS), F32),
            pltpu.VMEM((16, 128), F32),
            pltpu.VMEM((128, DEV * CAP), BF),
            pltpu.VMEM((16, DEV * CAP), F32),
            pltpu.VMEM((32, 1, 128), F32),
            pltpu.VMEM((DEV, 1, 128), F32),
            pltpu.VMEM((128, DEV), F32),
            dma, dma((16,)), dma, dma((16,)), dma((4,)), dma((4, CHUNKS)), dma((4,)), dma((4,)), dma, dma,
        ],
        compiler_params=pltpu.CompilerParams(
            collective_id=0, has_side_effects=True, vmem_limit_bytes=62 * 1024 * 1024
        ),
        cost_estimate=pl.CostEstimate(flops=12 * 10**9, bytes_accessed=1 << 20, transcendentals=2048),
    )(embeddings, cluster_id.reshape(1, ROWS), member_rank.reshape(1, ROWS), cluster_size, cluster_owner)
    return result.reshape(ROWS)


def solution(mesh):
    in_specs = (P(("dp", "narrow"), None), P(("dp", "narrow")), P(("dp", "narrow")), P(), P())
    out_specs = P(("dp", "narrow"))
    return jax.shard_map(shards, mesh=mesh, in_specs=in_specs, out_specs=out_specs, check_vma=False)
```
